256 devices in a mesh: band: 64 (over x, z, core), grp: 4 (over y).
Axes of the slice: x: 4, y: 4, z: 8, core: 2. Of those that a mesh axis runs over, the one named last changes fastest.
Arguments:
- stick_data: bfloat16 [192, 64, 6400], P('band'), may hold values from -6 to 6
- row_lengths: int32 [64], replicated, may hold values from 1 to 3, 80 in all
- row_order: int32 [80], replicated, may hold values from 0 to 79, each once
- source_order: int32 [64], replicated, may hold values from 0 to 63, each once
Outputs:
- exchange_sticks: bfloat16 [192, 64, 6400], P('band')
The draws below stay inside these ranges and needn't reach their ends.
Inputs may be any that keep to these rules, and one draw needn't show every extreme that they name: `row_lengths`: counts of G-stick rows per device sum to 80; the busiest device holds exactly 3. `row_order`: each G-stick row appears once. `source_order`: each orbital appears once; group g takes the entries g * 4 to g * 4 + 3.
All inputs are finite; a program needn't handle non-finite values.
Results may differ from the reference program's by a relative error of at most 0.019.
Values may be sent and summed in bfloat16 or wider, within the bound.
No kernel may reach another device: no remote copies, remote signals or barrier semaphores. Data moves between devices by JAX's collectives and lax.ppermute only.
A program may use at most 64 MiB of HBM per device.

```python
import math
import jax
import jax.numpy as jnp
import numpy as np
from jax import lax

NGX = 80
NGY = 80
NGZ = 80
SRC = 4
CAP = 3
ORB = 64
PLANE = 6400
N_BAND = 64
N_GRP = 4


def level_of(rng, shape, pieces, low, top_value):
    def one(dim, parts):
        steps = jax.random.uniform(jax.random.fold_in(jax.random.fold_in(rng, 6), dim), (parts,), jnp.float32, low / len(pieces), top_value / len(pieces))
        return jnp.repeat(jnp.exp(steps), shape[dim] // parts).reshape((-1,) + (1,) * (len(shape) - dim - 1))

    level = one(*pieces[0])
    for cut in pieces[1:]:
        level = level * one(*cut)
    return level


def length_profile(count, total, bound, lean):
    portions = [(1 << 20) // math.isqrt(standing ** lean) + 1 for standing in range(2, count + 1)]
    surplus, given = total - bound - (count - 1), [1] * (count - 1)
    while surplus > 0:
        candidates = [i for i in range(count - 1) if given[i] < bound]
        pool, left = sum([portions[i] for i in candidates]), surplus
        for i in candidates:
            addition = min(bound - given[i], max(1, left * portions[i] // pool), surplus)
            given[i] = given[i] + addition
            surplus = surplus - addition
    return np.array([bound] + given)


def uneven_parts(own_key, number_of, total, reach, skew):
    if number_of == 2:
        one = jax.random.randint(own_key, (), max(1, total - reach), min(reach, total - 1) + 1)
        return jnp.stack([one, total - one])
    sizes = jnp.asarray(length_profile(number_of, total, reach, skew), jnp.int32)
    pairs = (number_of - 1) // 2
    donor, sink = sizes[1:1 + 2 * pairs:2], sizes[2:2 + 2 * pairs:2]
    margin = jnp.minimum(donor - 1, reach - sink)
    moved = jax.random.randint(jax.random.fold_in(own_key, 1), (pairs,), 0, 1 << 20) % (margin + 1)
    sizes = sizes.at[1:1 + 2 * pairs:2].set(donor - moved).at[2:2 + 2 * pairs:2].set(sink + moved)
    return sizes[jax.random.permutation(jax.random.fold_in(own_key, 2), number_of)]


def centred(key, dims, width, limit, shards=(), kind=jnp.bfloat16):
    level = level_of(key, dims, shards, -0.22, 0.18) if shards else 1.0
    entries = jax.random.normal(key, dims, jnp.float32) * width * level
    return jnp.minimum(jnp.maximum(entries, -limit), limit).astype(kind)


def setup_inputs(seed: int = 0) -> dict:
    splits = jax.random.split(jax.random.key(seed), 5)
    return {
        "stick_data": centred(splits[0], (N_BAND * CAP, ORB, PLANE), 1.0, 6.0, ((0, 64),)),
        "row_lengths": uneven_parts(splits[1], N_BAND, NGX, CAP, 2).astype(jnp.int32),
        "row_order": jax.random.permutation(splits[2], NGX).astype(jnp.int32),
        "source_order": jax.random.permutation(splits[3], ORB).astype(jnp.int32),
    }


coulomb_peak = 4.0
screen_square = 64.0

def hartley(length):
    indices = jnp.arange(length, dtype=jnp.int32)
    product = indices[:, None] * indices[None, :] % length
    angles = product.astype(jnp.float32) * (2.0 * math.pi / length)
    return ((jnp.cos(angles) + jnp.sin(angles)) / math.sqrt(length)).astype(jnp.bfloat16)

def folded(length):
    indices = jnp.arange(length, dtype=jnp.int32)
    return jnp.minimum(indices, length - indices).astype(jnp.float32)

def screen_kernel():
    freq_x = folded(NGX)
    freq_y = folded(NGY)
    freq_z = folded(NGZ)
    square = (freq_x * freq_x)[:, None, None] + (freq_y * freq_y)[None, :, None] + (freq_z * freq_z)[None, None, :]
    return coulomb_peak / (1.0 + square / screen_square)

def transform(values, tables, keep_float):
    table_x, table_y, table_z = tables
    values = jnp.einsum('kx,bxyz->bkyz', table_x.astype(jnp.float32), values.astype(jnp.float32)).astype(jnp.bfloat16)
    values = jnp.einsum('ky,bxyz->bxkz', table_y.astype(jnp.float32), values.astype(jnp.float32)).astype(jnp.bfloat16)
    values = jnp.einsum('kz,bxyz->bxyk', table_z.astype(jnp.float32), values.astype(jnp.float32))
    if keep_float:
        return values
    return values.astype(jnp.bfloat16)

def reference(stick_data, row_lengths, row_order, source_order):
    slot_count = N_BAND * CAP
    slot_index = jnp.arange(slot_count, dtype=jnp.int32)
    owner_band = slot_index // CAP
    within = slot_index % CAP
    starts = (jnp.cumsum(row_lengths) - row_lengths).astype(jnp.int32)
    is_live = within < row_lengths[owner_band]
    position = jnp.clip(starts[owner_band] + within, 0, NGX - 1).astype(jnp.int32)
    row_of_slot = row_order[position]
    target_rows = jnp.where(is_live, row_of_slot, NGX).astype(jnp.int32)
    slot_of_row = jnp.zeros((NGX,), jnp.int32).at[target_rows].set(slot_index, mode='drop')
    coeffs = stick_data[slot_of_row]
    coeffs = jnp.transpose(coeffs, (1, 0, 2)).reshape(ORB, NGX, NGY, NGZ)
    tables = (hartley(NGX), hartley(NGY), hartley(NGZ))
    kernel = screen_kernel()
    orbitals = lax.map(lambda single: transform(single[None], tables, False)[0], coeffs)
    chosen = orbitals[source_order[:N_GRP * SRC]].reshape(N_GRP, SRC, NGX, NGY, NGZ)

    def act_on(target):
        summed = jnp.zeros((NGX, NGY, NGZ), jnp.float32)
        for group_index in range(N_GRP):
            partial_value = jnp.zeros((NGX, NGY, NGZ), jnp.float32)
            for source_slot in range(SRC):
                source = chosen[group_index, source_slot]
                density = (target.astype(jnp.float32) * source.astype(jnp.float32)).astype(jnp.bfloat16)
                spectrum = transform(density[None], tables, False)
                filtered = (kernel[None] * spectrum.astype(jnp.float32)).astype(jnp.bfloat16)
                potential = transform(filtered, tables, False)[0]
                partial_value = partial_value + source.astype(jnp.float32) * potential.astype(jnp.float32)
            summed = summed + transform(partial_value.astype(jnp.bfloat16)[None], tables, True)[0]
        return summed.astype(jnp.bfloat16)
    applied = lax.map(act_on, orbitals)
    flattened = applied.reshape(ORB, NGX, NGY * NGZ)
    picked = jnp.transpose(flattened[:, row_of_slot, :], (1, 0, 2))
    return jnp.where(is_live[:, None, None], picked, jnp.zeros_like(picked))
```

```python
import math

import jax
import jax.numpy as jnp
import numpy as np
from jax import lax
from jax.experimental import pallas as pl
from jax.experimental.pallas import tpu as pltpu
from jax.sharding import PartitionSpec as P

N = 80
LANES = 128
TILES = 50
QUART = 13
SRC = 4
SLOTS = 3
BANDS = 64
GROUPS = 4
ROWS_T = 40
ROWS_S = 16
PITCH = 80
BF = jnp.bfloat16
F32 = jnp.float32

coulomb_peak = 4.0
screen_square = 64.0


def hartley_table():
    index = np.arange(N)
    angles = (index[:, None] * index[None, :] % N).astype(np.float32) * np.float32(2.0 * math.pi / N)
    return ((np.cos(angles) + np.sin(angles)) / np.float32(math.sqrt(N))).astype(BF)


def expand_tables(table):
    out = np.zeros((4, 256, 256), BF)
    for p in range(4):
        off = 160 * p % LANES
        out[p, off : off + N, :N] = table
        out[p, off + N : off + 2 * N, LANES : LANES + N] = table
    return out


def pair_table(table):
    out = np.zeros((256, 256), BF)
    out[:N, :N] = table
    out[LANES : LANES + N, LANES : LANES + N] = table
    return out


def compress_tables(table):
    whole = np.zeros((1024, 640), BF)
    for y in range(8):
        whole[y * LANES : y * LANES + N, y * N : (y + 1) * N] = table
    return whole[:512, :256].copy(), whole[384:896, 256:512].copy(), whole[768:, 512:].copy()


def screen_table():
    freq = np.minimum(np.arange(N), N - np.arange(N)).astype(np.float32)
    sq = freq * freq
    total = sq[:41, None, None] + sq[None, :, None] + sq[None, None, :]
    out = np.zeros((41, N, LANES), np.float32)
    out[:, :, :N] = np.float32(coulomb_peak) / (np.float32(1.0) + total / np.float32(screen_square))
    return out


def dot(a, b):
    return jnp.dot(a, b, preferred_element_type=F32)


def dot_tn(a, b):
    return lax.dot_general(a, b, (((0,), (0,)), ((), ())), preferred_element_type=F32)


def pack_kernel(order_s, stick, lengths, order_v, table, msg_t, msg_s, sel, sel_t, scr, scr_s):
    g = lax.axis_index("grp")
    lens = lengths[...]
    d0 = lax.broadcasted_iota(jnp.int32, (BANDS, BANDS), 0)
    d1 = lax.broadcasted_iota(jnp.int32, (BANDS, BANDS), 1)
    before = jnp.where(d0 < d1, 1.0, 0.0).astype(BF)
    lens8 = jnp.broadcast_to(lens, (8, BANDS)).astype(F32)
    starts = dot(lens8.astype(BF), before)[:1]
    q0 = lax.broadcasted_iota(jnp.int32, (N, N), 0)
    perm = jnp.where(jnp.broadcast_to(order_v[...], (N, N)) == q0, 1.0, 0.0).astype(BF)
    permuted = dot(table[...], perm).astype(BF)
    place = lax.broadcasted_iota(jnp.int32, (N, BANDS), 0).astype(F32)
    for c in range(SLOTS):
        hit = (place == jnp.broadcast_to(starts + c, (N, BANDS))) & (
            jnp.broadcast_to(lens8[:1], (N, BANDS)) > c
        )
        one = jnp.where(hit, 1.0, 0.0).astype(BF)
        sel[c] = dot(permuted, one).astype(BF)
        sel_t[c] = lax.dot_general(
            one, permuted, (((0,), (1,)), ((), ())), preferred_element_type=F32
        ).astype(BF)
    first = QUART * g
    for c in range(SLOTS):

        def body(t, _):
            lane = pl.multiple_of(jnp.minimum(first + t, TILES - 1) * LANES, LANES)
            row = pl.multiple_of((c * QUART + t) * BANDS, BANDS)
            scr[pl.ds(row, BANDS), :] = stick[c, :, pl.ds(lane, LANES)].astype(F32)
            return 0

        lax.fori_loop(0, QUART, body, 0, unroll=True)

    def out_body(b, _):
        msg_t[b] = scr[pl.ds(b, ROWS_T, stride=BANDS), :].astype(BF)
        return 0

    lax.fori_loop(0, BANDS, out_body, 0, unroll=8)
    b1 = lax.broadcasted_iota(jnp.int32, (16, BANDS), 1)
    r1 = lax.broadcasted_iota(jnp.int32, (16, BANDS), 0)
    pick = jnp.zeros((16, BANDS), F32)
    for k in range(SRC):
        pick = jnp.where((r1 == k) & (b1 == order_s[g * SRC + k]), 1.0, pick)
    pick = pick.astype(BF)
    for c in range(SLOTS):
        for u in range(TILES // 2):
            got = dot(pick, stick[c, :, u * 256 : u * 256 + 256])
            for h in range(2):
                row = (2 * u + h) * ROWS_S + c * SRC
                scr_s[row : row + SRC, :] = got[:SRC, h * LANES : (h + 1) * LANES]
    for t in range(TILES):
        msg_s[t] = scr_s[t * ROWS_S : (t + 1) * ROWS_S, :].astype(BF)


def rows_kernel(got_t, got_s, sel, quarter, piece, scr, scr_s):
    def load(d, _):
        scr[pl.ds(pl.multiple_of(d * ROWS_T, 8), ROWS_T), :] = got_t[d].astype(F32)
        scr_s[pl.ds(pl.multiple_of(d * ROWS_S, 8), ROWS_S), :] = got_s[d].astype(F32)
        return 0

    lax.fori_loop(0, BANDS, load, 0, unroll=8)
    tables = [sel[c] for c in range(SLOTS)]
    for t in range(QUART):
        total = jnp.zeros((N, LANES), F32)
        for c in range(SLOTS):
            rows = scr[pl.ds(c * QUART + t, BANDS, stride=ROWS_T), :].astype(BF)
            total = total + dot(tables[c], rows)
        quarter[t] = total.astype(BF)
    for k in range(SRC):
        total = jnp.zeros((N, LANES), F32)
        for c in range(SLOTS):
            rows = scr_s[pl.ds(c * SRC + k, BANDS, stride=ROWS_S), :].astype(BF)
            total = total + dot(tables[c], rows)
        piece[k] = total.astype(BF)


def turned(scr, index):
    return jnp.concatenate(
        [
            scr[pl.ds(index, N, stride=PITCH), :].astype(BF),
            scr[pl.ds(index + 1, N, stride=PITCH), :].astype(BF),
        ],
        axis=1,
    )


def put(scr, index, values):
    scr[pl.ds(pl.multiple_of(index * PITCH, 8), N), :] = values[:, :LANES]
    scr[pl.ds(pl.multiple_of(index * PITCH + PITCH, 8), N), :] = values[:, LANES:]


def to_real(tile, out, table, expand, scr):
    def z_body(i, _):
        for p in range(4):
            a = i * 5 + (160 * p) // LANES
            both = jnp.concatenate([tile(a), tile(a + 1)], axis=1)
            put(scr, i * 8 + 2 * p, dot(both, expand[p]))
        return 0

    lax.fori_loop(0, 10, z_body, 0)
    h = table[...]

    def y_body(i, _):
        for p in range(4):
            x = i * 8 + 2 * p
            res = dot(h, turned(scr, x)).astype(BF)
            out[x] = res[:, :LANES]
            out[x + 1] = res[:, LANES:]
        return 0

    lax.fori_loop(0, 10, y_body, 0)


def pairs_kernel(
    quarters, same_core, other_core, table, expand, twin, c0, c1, c2, screen,
    out0, out1, out2, out3,
    target, source, partial, scr_a, scr_b, final, pieces,
):
    g = lax.axis_index("grp")
    band = lax.axis_index("band")
    core, z_at, x_at = band & 1, (band >> 1) & 7, band >> 4
    for kx in range(4):
        for kz in range(8):
            origin = (((x_at - kx) & 3) * 8 + ((z_at - kz) & 7)) * 2
            pieces[origin + core] = same_core[kx, kz]
            pieces[origin + 1 - core] = other_core[kx, kz]
    h = table[...]

    def target_tile(t):
        return quarters[t]

    to_real(target_tile, target, table, expand, scr_a)

    for k in range(SRC):

        def source_tile(t):
            return pieces[t, k]

        to_real(source_tile, source, table, expand, scr_a)

        def density_body(i, _):
            for p in range(4):
                x = i * 8 + 2 * p
                dens = jnp.concatenate(
                    [target[x] * source[x], target[x + 1] * source[x + 1]], axis=1
                )
                put(scr_a, x, dot(dot(h, dens).astype(BF), twin[...]))
            return 0

        lax.fori_loop(0, 10, density_body, 0)

        def filter_body(i, _):
            for p in range(4):
                y = i * 8 + 2 * p
                spec = dot(h, turned(scr_a, y))
                y0 = jnp.minimum(y, N - y)
                y1 = jnp.minimum(y + 1, N - 1 - y)
                weight = jnp.concatenate([screen[y0], screen[y1]], axis=1)
                put(scr_b, y, dot(h, (spec * weight).astype(BF)))
            return 0

        lax.fori_loop(0, 10, filter_body, 0)

        def potential_body(i, _):
            for p in range(4):
                x = i * 8 + 2 * p
                pot = dot(h, dot(turned(scr_b, x), twin[...]).astype(BF))
                for e in range(2):
                    term = source[x + e].astype(F32) * pot[:, e * LANES : (e + 1) * LANES]
                    if k == 0:
                        partial[x + e] = term
                    else:
                        partial[x + e] = partial[x + e] + term
            return 0

        lax.fori_loop(0, 10, potential_body, 0)

    def last_y_body(i, _):
        for p in range(4):
            x = i * 8 + 2 * p
            both = jnp.concatenate([partial[x].astype(BF), partial[x + 1].astype(BF)], axis=1)
            put(scr_a, x, dot(h, both))
        return 0

    lax.fori_loop(0, 10, last_y_body, 0)

    def last_z_body(i, _):
        y = i * 8
        eight = jnp.concatenate([turned(scr_a, y + 2 * p) for p in range(4)], axis=1)
        r0 = dot(eight[:, :512], c0[...]).astype(BF)
        r1 = dot(eight[:, 384:896], c1[...]).astype(BF)
        r2 = dot(eight[:, 768:], c2[...]).astype(BF)
        t = i * 5
        final[t] = r0[:, :LANES]
        final[t + 1] = r0[:, LANES:]
        final[t + 2] = r1[:, :LANES]
        final[t + 3] = r1[:, LANES:]
        final[t + 4] = r2
        return 0

    lax.fori_loop(0, 10, last_z_body, 0)
    final[TILES] = jnp.zeros((N, LANES), BF)
    final[TILES + 1] = jnp.zeros((N, LANES), BF)
    for k, out in enumerate((out0, out1, out2, out3)):
        start = ((g + k) & 3) * QUART
        for t in range(QUART):
            out[t] = final[start + t]


def select_kernel(own, got1, got2, got3, sel_t, msg, scr):
    tables = [sel_t[c] for c in range(SLOTS)]
    for t in range(QUART):
        total = (
            own[t].astype(F32) + got1[t].astype(F32) + got2[t].astype(F32) + got3[t].astype(F32)
        ).astype(BF)
        for c in range(SLOTS):
            scr[(c * QUART + t) * BANDS : (c * QUART + t + 1) * BANDS, :] = dot(tables[c], total)

    def body(d, _):
        msg[d] = scr[pl.ds(d, ROWS_T, stride=BANDS), :].astype(BF)
        return 0

    lax.fori_loop(0, BANDS, body, 0, unroll=8)


def rows_out_kernel(got, out, scr):
    def load(b, _):
        scr[pl.ds(pl.multiple_of(b * ROWS_T, 8), ROWS_T), :] = got[b].astype(F32)
        return 0

    lax.fori_loop(0, BANDS, load, 0, unroll=8)
    for c in range(SLOTS):
        for t in range(QUART):
            out[c, :, t * LANES : (t + 1) * LANES] = scr[
                pl.ds(c * QUART + t, BANDS, stride=ROWS_T), :
            ].astype(BF)


def join_kernel(own, got1, got2, got3, out):
    g = lax.axis_index("grp")
    wide = QUART * LANES
    short = (TILES - 3 * QUART) * LANES
    for k, ref in enumerate((own, got1, got2, got3)):
        origin = (g - k) & 3
        start = pl.multiple_of(origin * wide, LANES)

        @pl.when(origin < 3)
        def _():
            for c in range(SLOTS):
                out[c, :, pl.ds(start, wide)] = ref[c]

        @pl.when(origin == 3)
        def _():
            for c in range(SLOTS):
                out[c, :, 3 * wide :] = ref[c, :, :short]


VM = pl.BlockSpec(memory_space=pltpu.VMEM)
SM = pl.BlockSpec(memory_space=pltpu.SMEM)
ANY = pl.BlockSpec(memory_space=pl.ANY)
PARAMS = pltpu.CompilerParams(vmem_limit_bytes=56 * 1024 * 1024)


def shape(dims, kind=BF):
    return jax.ShapeDtypeStruct(dims, kind)


def shift_grp(value, k):
    return lax.ppermute(value, "grp", [(i, (i + k) % GROUPS) for i in range(GROUPS)])


def shift_band(value, dx, dz, dc):
    moves = []
    for x in range(4):
        for z in range(8):
            for c in range(2):
                there = (((x + dx) % 4) * 8 + (z + dz) % 8) * 2 + (c + dc) % 2
                moves.append(((x * 8 + z) * 2 + c, there))
    return lax.ppermute(value, "band", moves)


def shards(stick_data, row_lengths, row_order, source_order):
    table = jnp.asarray(hartley_table())
    expand = jnp.asarray(expand_tables(hartley_table()))
    twin = jnp.asarray(pair_table(hartley_table()))
    c0, c1, c2 = (jnp.asarray(v) for v in compress_tables(hartley_table()))
    screen = jnp.asarray(screen_table())

    msg_t, msg_s, sel, sel_t = pl.pallas_call(
        pack_kernel,
        out_shape=(
            shape((BANDS, ROWS_T, LANES)),
            shape((BANDS, ROWS_S, LANES)),
            shape((SLOTS, N, BANDS)),
            shape((SLOTS, BANDS, N)),
        ),
        in_specs=[SM, VM, VM, VM, VM],
        out_specs=(VM, VM, VM, VM),
        scratch_shapes=[
            pltpu.VMEM((ROWS_T * BANDS, LANES), F32),
            pltpu.VMEM((TILES * ROWS_S, LANES), F32),
        ],
        compiler_params=PARAMS,
    )(source_order, stick_data, row_lengths.reshape(1, BANDS), row_order.reshape(1, N), table)

    got_s = lax.all_to_all(msg_s, "band", 0, 0, tiled=True)
    got_t = lax.all_to_all(msg_t, "band", 0, 0, tiled=True)

    quarter, piece = pl.pallas_call(
        rows_kernel,
        out_shape=(shape((QUART, N, LANES)), shape((SRC, N, LANES))),
        in_specs=[VM, VM, VM],
        out_specs=(VM, VM),
        scratch_shapes=[
            pltpu.VMEM((ROWS_T * BANDS, LANES), F32),
            pltpu.VMEM((ROWS_S * BANDS, LANES), F32),
        ],
        compiler_params=PARAMS,
    )(got_t, got_s, sel)

    quarters = lax.all_gather(quarter, "grp", axis=0, tiled=True)
    along_z = jnp.stack([piece] + [shift_band(piece, 0, k, 0) for k in range(1, 8)])
    along_x = jnp.stack([along_z] + [shift_band(along_z, k, 0, 0) for k in range(1, 4)])
    twins = shift_band(along_x, 0, 0, 1)

    outs = pl.pallas_call(
        pairs_kernel,
        out_shape=tuple(shape((QUART, N, LANES)) for _ in range(4)),
        in_specs=[VM] * 10,
        out_specs=(VM,) * 4,
        scratch_shapes=[
            pltpu.VMEM((N, N, LANES), BF),
            pltpu.VMEM((N, N, LANES), BF),
            pltpu.VMEM((N, N, LANES), F32),
            pltpu.VMEM((N * PITCH, LANES), F32),
            pltpu.VMEM((N * PITCH, LANES), F32),
            pltpu.VMEM((TILES + 2, N, LANES), BF),
            pltpu.VMEM((BANDS, SRC, N, LANES), BF),
        ],
        compiler_params=PARAMS,
    )(quarters, along_x, twins, table, expand, twin, c0, c1, c2, screen)

    parts = [outs[0]] + [shift_grp(outs[k], k) for k in range(1, 4)]
    message = pl.pallas_call(
        select_kernel,
        out_shape=shape((BANDS, ROWS_T, LANES)),
        in_specs=[VM] * 5,
        out_specs=VM,
        scratch_shapes=[pltpu.VMEM((ROWS_T * BANDS, LANES), F32)],
        compiler_params=PARAMS,
    )(*parts, sel_t)

    received = lax.all_to_all(message, "band", 0, 0, tiled=True)
    rows = pl.pallas_call(
        rows_out_kernel,
        out_shape=shape((SLOTS, BANDS, QUART * LANES)),
        in_specs=[VM],
        out_specs=VM,
        scratch_shapes=[pltpu.VMEM((ROWS_T * BANDS, LANES), F32)],
        compiler_params=PARAMS,
    )(received)

    others = [shift_grp(rows, k) for k in range(1, 4)]
    return pl.pallas_call(
        join_kernel,
        out_shape=shape((SLOTS, BANDS, TILES * LANES)),
        in_specs=[VM] * 4,
        out_specs=VM,
        compiler_params=PARAMS,
    )(rows, *others)


def solution(mesh):
    return jax.shard_map(
        shards,
        mesh=mesh,
        in_specs=(P("band", None, None), P(), P(), P()),
        out_specs=P("band", None, None),
        check_vma=False,
    )
```

```python
import functools
import math

import jax
import jax.numpy as jnp
import numpy as np
from jax import lax
from jax.experimental import pallas as pl
from jax.experimental.pallas import tpu as pltpu
from jax.sharding import PartitionSpec as P

N = 80
LANES = 128
TILES = 50
QUART = 13
SRC = 4
SLOTS = 3
BANDS = 64
GROUPS = 4
ROWS_T = 40
ROWS_S = 16
ROWS_M = ROWS_T + ROWS_S
HALF = BANDS // 2
PITCH = 88
BF = jnp.bfloat16
F32 = jnp.float32

coulomb_peak = 4.0
screen_square = 64.0


def hartley_table():
    index = np.arange(N)
    angles = (index[:, None] * index[None, :] % N).astype(np.float32) * np.float32(2.0 * math.pi / N)
    return ((np.cos(angles) + np.sin(angles)) / np.float32(math.sqrt(N))).astype(BF)


def expand_tables(table):
    out = np.zeros((4, 256, 256), BF)
    for p in range(4):
        off = 160 * p % LANES
        out[p, off : off + N, :N] = table
        out[p, off + N : off + 2 * N, LANES : LANES + N] = table
    return out


def pair_table(table):
    out = np.zeros((256, 256), BF)
    out[:N, :N] = table
    out[LANES : LANES + N, LANES : LANES + N] = table
    return out


def compress_tables(table):
    whole = np.zeros((1024, 640), BF)
    for y in range(8):
        whole[y * LANES : y * LANES + N, y * N : (y + 1) * N] = table
    return whole[:512, :256].copy(), whole[384:896, 256:512].copy(), whole[768:, 512:].copy()


def screen_table():
    freq = np.minimum(np.arange(N), N - np.arange(N)).astype(np.float32)
    sq = freq * freq
    total = sq[:41, None, None] + sq[None, :, None] + sq[None, None, :]
    out = np.zeros((41, N, LANES), np.float32)
    out[:, :, :N] = np.float32(coulomb_peak) / (np.float32(1.0) + total / np.float32(screen_square))
    return out


def dot(a, b):
    return jnp.dot(a, b, preferred_element_type=F32)


def dot_tn(a, b):
    return lax.dot_general(a, b, (((0,), (0,)), ((), ())), preferred_element_type=F32)


def pack_kernel(order_s, stick, lengths, order_v, table, msg, sel, sel_t, scr, scr_s):
    g = lax.axis_index("grp")
    lens = lengths[...]
    d0 = lax.broadcasted_iota(jnp.int32, (BANDS, BANDS), 0)
    d1 = lax.broadcasted_iota(jnp.int32, (BANDS, BANDS), 1)
    before = jnp.where(d0 < d1, 1.0, 0.0).astype(BF)
    lens8 = jnp.broadcast_to(lens, (8, BANDS)).astype(F32)
    starts = dot(lens8.astype(BF), before)[:1]
    q0 = lax.broadcasted_iota(jnp.int32, (N, N), 0)
    perm = jnp.where(jnp.broadcast_to(order_v[...], (N, N)) == q0, 1.0, 0.0).astype(BF)
    permuted = dot(table[...], perm).astype(BF)
    place = lax.broadcasted_iota(jnp.int32, (N, BANDS), 0).astype(F32)
    for c in range(SLOTS):
        hit = (place == jnp.broadcast_to(starts + c, (N, BANDS))) & (
            jnp.broadcast_to(lens8[:1], (N, BANDS)) > c
        )
        one = jnp.where(hit, 1.0, 0.0).astype(BF)
        sel[c] = dot(permuted, one).astype(BF)
        sel_t[c] = lax.dot_general(
            one, permuted, (((0,), (1,)), ((), ())), preferred_element_type=F32
        ).astype(BF)
    first = QUART * g
    for c in range(SLOTS):

        def body(t, _):
            lane = pl.multiple_of(jnp.minimum(first + t, TILES - 1) * LANES, LANES)
            row = pl.multiple_of((c * QUART + t) * BANDS, BANDS)
            scr[pl.ds(row, BANDS), :] = stick[c, :, pl.ds(lane, LANES)].astype(F32)
            return 0

        lax.fori_loop(0, QUART, body, 0, unroll=True)

    b1 = lax.broadcasted_iota(jnp.int32, (16, BANDS), 1)
    r1 = lax.broadcasted_iota(jnp.int32, (16, BANDS), 0)
    pick = jnp.zeros((16, BANDS), F32)
    for k in range(SRC):
        pick = jnp.where((r1 == k) & (b1 == order_s[g * SRC + k]), 1.0, pick)
    pick = pick.astype(BF)
    for c in range(SLOTS):
        for u in range(TILES // 2):
            got = dot(pick, stick[c, :, u * 256 : u * 256 + 256])
            for h in range(2):
                row = (2 * u + h) * ROWS_S + c * SRC
                scr_s[row : row + SRC, :] = got[:SRC, h * LANES : (h + 1) * LANES]

    def out_body(b, _):
        mine = scr[pl.ds(b, ROWS_T, stride=BANDS), :]
        tile = scr_s[pl.ds(pl.multiple_of(b * ROWS_S, 8), ROWS_S), :]
        msg[b] = jnp.concatenate([mine, tile], axis=0).astype(BF)
        return 0

    lax.fori_loop(0, BANDS, out_body, 0, unroll=8)


def rows_kernel(got, sel, quarter, piece, scr):
    def load(d, _):
        scr[pl.ds(pl.multiple_of(d * ROWS_M, 8), ROWS_M), :] = got[d].astype(F32)
        return 0

    lax.fori_loop(0, BANDS, load, 0, unroll=8)
    tables = [sel[c] for c in range(SLOTS)]
    for out, count, first in ((piece, SRC, ROWS_T), (quarter, QUART, 0)):
        for t in range(count):
            total = jnp.zeros((N, LANES), F32)
            for c in range(SLOTS):
                rows = scr[pl.ds(first + c * count + t, BANDS, stride=ROWS_M), :].astype(BF)
                total = total + dot(tables[c], rows)
            out[t] = total.astype(BF)


def turned(scr, index):
    return jnp.concatenate(
        [
            scr[pl.ds(index, N, stride=PITCH), :].astype(BF),
            scr[pl.ds(index + 1, N, stride=PITCH), :].astype(BF),
        ],
        axis=1,
    )


def put(scr, index, values):
    scr[index * PITCH : index * PITCH + N, :] = values[:, :LANES]
    scr[(index + 1) * PITCH : (index + 1) * PITCH + N, :] = values[:, LANES:]


def side(ref, index):
    return jnp.concatenate([ref[index], ref[index + 1]], axis=1)


CHUNK = 5


def to_real(tile, out, table, expand, scr):
    for p in range(4):
        for lead in range(0, 10, CHUNK):
            rows = []
            for i in range(lead, lead + CHUNK):
                a = i * 5 + (160 * p) // LANES
                rows.append(jnp.concatenate([tile(a), tile(a + 1)], axis=1))
            res = dot(jnp.concatenate(rows, axis=0), expand[p])
            for j in range(CHUNK):
                put(scr, (lead + j) * 8 + 2 * p, res[j * N : (j + 1) * N])
    h = table[...]
    for x in range(0, N, 2):
        res = dot(h, turned(scr, x)).astype(BF)
        out[x] = res[:, :LANES]
        out[x + 1] = res[:, LANES:]


def target_kernel(own, got1, got2, got3, table, expand, out, scr, quarters):
    g = lax.axis_index("grp")
    for k, ref in enumerate((own, got1, got2, got3)):
        start = ((g - k) & 3) * QUART
        for t in range(QUART):
            quarters[start + t] = ref[t]
    to_real(lambda t: quarters[t], out, table, expand, scr)


def gather_tiles(same_core, other_core, pieces):
    band = lax.axis_index("band")
    core, z_at, x_at = band & 1, (band >> 1) & 7, band >> 4
    for kx in range(4):
        for kz in range(8):
            origin = (((x_at - kx) & 3) * 8 + ((z_at - kz) & 7)) * 2
            for e in range(2):
                pieces[origin + core, 2 * e : 2 * e + 2] = same_core[2 * kx + e][kz]
                pieces[origin + 1 - core, 2 * e : 2 * e + 2] = other_core[2 * kx + e][kz]


def one_source(pieces, k, target, source, partial, table, expand, twin, screen, scr_a, scr_b):
    to_real(lambda t: pieces[t, k], source, table, expand, scr_a)
    h = table[...]
    turn = twin[...]
    for lead in range(0, N, 2 * CHUNK):
        rows = []
        for x in range(lead, lead + 2 * CHUNK, 2):
            rows.append(dot(h, side(target, x) * side(source, x)).astype(BF))
        res = dot(jnp.concatenate(rows, axis=0), turn)
        for j in range(CHUNK):
            put(scr_a, lead + 2 * j, res[j * N : (j + 1) * N])
    for y in range(0, N, 2):
        spec = dot(h, turned(scr_a, y))
        weight = jnp.concatenate([screen[min(y, N - y)], screen[min(y + 1, N - 1 - y)]], axis=1)
        put(scr_b, y, dot(h, (spec * weight).astype(BF)))
    for lead in range(0, N, 2 * CHUNK):
        rows = [turned(scr_b, x) for x in range(lead, lead + 2 * CHUNK, 2)]
        res = dot(jnp.concatenate(rows, axis=0), turn).astype(BF)
        for j in range(CHUNK):
            pot = dot(h, res[j * N : (j + 1) * N])
            for e in range(2):
                x = lead + 2 * j + e
                term = source[x].astype(F32) * pot[:, e * LANES : (e + 1) * LANES]
                partial[x] = partial[x] + term


def last_transform(partial, table, c0, c1, c2, scr, final):
    h = table[...]
    for x in range(0, N, 2):
        put(scr, x, dot(h, side(partial, x).astype(BF)))
    blocks = [[turned(scr, y + 2 * p) for p in range(4)] for y in range(0, N, 8)]
    for i in range(0, 10, CHUNK):
        eights = [jnp.concatenate(blocks[i + j], axis=1) for j in range(CHUNK)]
        r0 = dot(jnp.concatenate([v[:, :512] for v in eights], axis=0), c0[...]).astype(BF)
        r1 = dot(jnp.concatenate([v[:, 384:896] for v in eights], axis=0), c1[...]).astype(BF)
        r2 = dot(jnp.concatenate([v[:, 768:] for v in eights], axis=0), c2[...]).astype(BF)
        for j in range(CHUNK):
            t = (i + j) * 5
            rows = slice(j * N, (j + 1) * N)
            final[t] = r0[rows, :LANES]
            final[t + 1] = r0[rows, LANES:]
            final[t + 2] = r1[rows, :LANES]
            final[t + 3] = r1[rows, LANES:]
            final[t + 4] = r2[rows]
    final[TILES] = jnp.zeros((N, LANES), BF)
    final[TILES + 1] = jnp.zeros((N, LANES), BF)


def pairs_kernel(*refs):
    same_core, other_core = refs[:8], refs[8:16]
    target, table, expand, twin, c0, c1, c2, screen = refs[16:24]
    outs = refs[24:28]
    source, partial, scr_a, scr_b, final, pieces = refs[28:]
    g = lax.axis_index("grp")
    gather_tiles(same_core, other_core, pieces)
    partial[...] = jnp.zeros_like(partial)

    def body(k, _):
        one_source(pieces, k, target, source, partial, table, expand, twin, screen, scr_a, scr_b)
        return 0

    lax.fori_loop(0, SRC, body, 0)
    last_transform(partial, table, c0, c1, c2, scr_a, final)
    for k, out in enumerate(outs):
        start = ((g + k) & 3) * QUART
        for t in range(QUART):
            out[t] = final[start + t]


def select_kernel(own, got1, got2, got3, sel_t, msg, scr):
    tables = [sel_t[c] for c in range(SLOTS)]
    for t in range(QUART):
        total = (
            own[t].astype(F32) + got1[t].astype(F32) + got2[t].astype(F32) + got3[t].astype(F32)
        ).astype(BF)
        for c in range(SLOTS):
            scr[(c * QUART + t) * BANDS : (c * QUART + t + 1) * BANDS, :] = dot(tables[c], total)

    def body(d, _):
        msg[d] = scr[pl.ds(d, ROWS_T, stride=BANDS), :].astype(BF)
        return 0

    lax.fori_loop(0, BANDS, body, 0, unroll=8)


def rows_out_kernel(got, low, high, scr):
    def load(b, _):
        scr[pl.ds(pl.multiple_of(b * ROWS_T, 8), ROWS_T), :] = got[b].astype(F32)
        return 0

    lax.fori_loop(0, BANDS, load, 0, unroll=8)
    for c in range(SLOTS):
        for t in range(QUART):
            rows = scr[pl.ds(c * QUART + t, BANDS, stride=ROWS_T), :].astype(BF)
            low[c, :, t * LANES : (t + 1) * LANES] = rows[:HALF]
            high[c, :, t * LANES : (t + 1) * LANES] = rows[HALF:]


def join_kernel(*refs):
    out = refs[8]
    g = lax.axis_index("grp")
    wide = QUART * LANES
    short = (TILES - 3 * QUART) * LANES
    for k in range(4):
        origin = (g - k) & 3
        start = pl.multiple_of(origin * wide, LANES)

        @pl.when(origin < 3)
        def _():
            for c in range(SLOTS):
                for e in range(2):
                    out[c, e * HALF : (e + 1) * HALF, pl.ds(start, wide)] = refs[2 * k + e][c]

        @pl.when(origin == 3)
        def _():
            for c in range(SLOTS):
                for e in range(2):
                    out[c, e * HALF : (e + 1) * HALF, 3 * wide :] = refs[2 * k + e][c, :, :short]


VM = pl.BlockSpec(memory_space=pltpu.VMEM)
SM = pl.BlockSpec(memory_space=pltpu.SMEM)
ANY = pl.BlockSpec(memory_space=pl.ANY)
PARAMS = pltpu.CompilerParams(vmem_limit_bytes=56 * 1024 * 1024)


def shape(dims, kind=BF):
    return jax.ShapeDtypeStruct(dims, kind)


def shift_grp(value, k):
    return lax.ppermute(value, "grp", [(i, (i + k) % GROUPS) for i in range(GROUPS)])


def shift_band(value, dx, dz, dc):
    moves = []
    for x in range(4):
        for z in range(8):
            for c in range(2):
                there = (((x + dx) % 4) * 8 + (z + dz) % 8) * 2 + (c + dc) % 2
                moves.append(((x * 8 + z) * 2 + c, there))
    return lax.ppermute(value, "band", moves)


def ring_gather(first, second, step):
    ahead = step(first, 1), step(second, 1)
    behind = step(first, 3), step(second, 3)
    far = step(ahead[0], 1), step(behind[1], 3)
    return [(first, second), ahead, far, behind]


def shards(stick_data, row_lengths, row_order, source_order):
    table = jnp.asarray(hartley_table())
    expand = jnp.asarray(expand_tables(hartley_table()))
    twin = jnp.asarray(pair_table(hartley_table()))
    c0, c1, c2 = (jnp.asarray(v) for v in compress_tables(hartley_table()))
    screen = jnp.asarray(screen_table())

    msg, sel, sel_t = pl.pallas_call(
        pack_kernel,
        out_shape=(
            shape((BANDS, ROWS_M, LANES)),
            shape((SLOTS, N, BANDS)),
            shape((SLOTS, BANDS, N)),
        ),
        in_specs=[SM, VM, VM, VM, VM],
        out_specs=(VM, VM, VM),
        scratch_shapes=[
            pltpu.VMEM((ROWS_T * BANDS, LANES), F32),
            pltpu.VMEM((BANDS * ROWS_S, LANES), F32),
        ],
        compiler_params=PARAMS,
    )(source_order, stick_data, row_lengths.reshape(1, BANDS), row_order.reshape(1, N), table)
    got = lax.all_to_all(msg, "band", 0, 0, tiled=True)
    quarter, piece = pl.pallas_call(
        rows_kernel,
        out_shape=(shape((QUART, N, LANES)), shape((SRC, N, LANES))),
        in_specs=[VM, VM],
        out_specs=(VM, VM),
        scratch_shapes=[pltpu.VMEM((ROWS_M * BANDS, LANES), F32)],
        compiler_params=PARAMS,
    )(got, sel)

    along_z = [piece] + [shift_band(piece, 0, k, 0) for k in range(1, 8)]
    quarters = [quarter] + [shift_grp(quarter, k) for k in range(1, 4)]
    halves = [jnp.stack([v[2 * e : 2 * e + 2] for v in along_z]) for e in range(2)]
    gathered = ring_gather(*halves, lambda v, k: shift_band(v, k, 0, 0))
    same_core = [v for both in gathered for v in both]
    other_core = [shift_band(v, 0, 0, 1) for v in same_core]

    target = pl.pallas_call(
        target_kernel,
        out_shape=shape((N, N, LANES)),
        in_specs=[VM] * 6,
        out_specs=VM,
        scratch_shapes=[
            pltpu.VMEM((N * PITCH, LANES), F32),
            pltpu.VMEM((4 * QUART, N, LANES), BF),
        ],
        compiler_params=PARAMS,
    )(*quarters, table, expand)

    outs = pl.pallas_call(
        pairs_kernel,
        out_shape=tuple(shape((QUART, N, LANES)) for _ in range(4)),
        in_specs=[VM] * 24,
        out_specs=(VM,) * 4,
        scratch_shapes=[
            pltpu.VMEM((N, N, LANES), BF),
            pltpu.VMEM((N, N, LANES), F32),
            pltpu.VMEM((N * PITCH, LANES), F32),
            pltpu.VMEM((N * PITCH, LANES), F32),
            pltpu.VMEM((TILES + 2, N, LANES), BF),
            pltpu.VMEM((BANDS, SRC, N, LANES), BF),
        ],
        compiler_params=PARAMS,
    )(*same_core, *other_core, target, table, expand, twin, c0, c1, c2, screen)

    parts = [outs[0]] + [shift_grp(outs[k], k) for k in range(1, 4)]
    message = pl.pallas_call(
        select_kernel,
        out_shape=shape((BANDS, ROWS_T, LANES)),
        in_specs=[VM] * 5,
        out_specs=VM,
        scratch_shapes=[pltpu.VMEM((ROWS_T * BANDS, LANES), F32)],
        compiler_params=PARAMS,
    )(*parts, sel_t)

    received = lax.all_to_all(message, "band", 0, 0, tiled=True)
    low, high = pl.pallas_call(
        rows_out_kernel,
        out_shape=(shape((SLOTS, HALF, QUART * LANES)),) * 2,
        in_specs=[VM],
        out_specs=(VM, VM),
        scratch_shapes=[pltpu.VMEM((ROWS_T * BANDS, LANES), F32)],
        compiler_params=PARAMS,
    )(received)

    spread = ring_gather(low, high, shift_grp)
    return pl.pallas_call(
        join_kernel,
        out_shape=shape((SLOTS, BANDS, TILES * LANES)),
        in_specs=[VM] * 8,
        out_specs=VM,
        compiler_params=PARAMS,
    )(*[v for both in spread for v in both])


def solution(mesh):
    return jax.shard_map(
        shards,
        mesh=mesh,
        in_specs=(P("band", None, None), P(), P(), P()),
        out_specs=P("band", None, None),
        check_vma=False,
    )
```

```python
import functools
import math

import jax
import jax.numpy as jnp
import numpy as np
from jax import lax
from jax.experimental import pallas as pl
from jax.experimental.pallas import tpu as pltpu
from jax.sharding import PartitionSpec as P

N = 80
LANES = 128
TILES = 50
QUART = 13
SRC = 4
SLOTS = 3
BANDS = 64
GROUPS = 4
ROWS_T = 40
ROWS_S = 16
EACH = 3
WHOLE = EACH * BANDS
REST = 10
PIECE = 256
ROWS_M = ROWS_T + ROWS_S
HALF = BANDS // 2
PITCH = 88
BF = jnp.bfloat16
F32 = jnp.float32

coulomb_peak = 4.0
screen_square = 64.0


def hartley_table():
    index = np.arange(N)
    angles = (index[:, None] * index[None, :] % N).astype(np.float32) * np.float32(2.0 * math.pi / N)
    return ((np.cos(angles) + np.sin(angles)) / np.float32(math.sqrt(N))).astype(BF)


def expand_tables(table):
    out = np.zeros((4, 256, 256), BF)
    for p in range(4):
        off = 160 * p % LANES
        out[p, off : off + N, :N] = table
        out[p, off + N : off + 2 * N, LANES : LANES + N] = table
    return out


def pair_table(table):
    out = np.zeros((256, 256), BF)
    out[:N, :N] = table
    out[LANES : LANES + N, LANES : LANES + N] = table
    return out


def compress_tables(table):
    whole = np.zeros((1024, 640), BF)
    for y in range(8):
        whole[y * LANES : y * LANES + N, y * N : (y + 1) * N] = table
    return whole[:512, :256].copy(), whole[384:896, 256:512].copy(), whole[768:, 512:].copy()


def screen_table():
    freq = np.minimum(np.arange(N), N - np.arange(N)).astype(np.float32)
    sq = freq * freq
    total = sq[:41, None, None] + sq[None, :, None] + sq[None, None, :]
    out = np.zeros((41, N, LANES), np.float32)
    out[:, :, :N] = np.float32(coulomb_peak) / (np.float32(1.0) + total / np.float32(screen_square))
    return out


def dot(a, b):
    return jnp.dot(a, b, preferred_element_type=F32)


def dot_tn(a, b):
    return lax.dot_general(a, b, (((0,), (0,)), ((), ())), preferred_element_type=F32)


def pack_kernel(order_s, stick, lengths, order_v, table, msg, sel, sel_t, scr, scr_s):
    g = lax.axis_index("grp")
    lens = lengths[...]
    d0 = lax.broadcasted_iota(jnp.int32, (BANDS, BANDS), 0)
    d1 = lax.broadcasted_iota(jnp.int32, (BANDS, BANDS), 1)
    before = jnp.where(d0 < d1, 1.0, 0.0).astype(BF)
    lens8 = jnp.broadcast_to(lens, (8, BANDS)).astype(F32)
    starts = dot(lens8.astype(BF), before)[:1]
    q0 = lax.broadcasted_iota(jnp.int32, (N, N), 0)
    perm = jnp.where(jnp.broadcast_to(order_v[...], (N, N)) == q0, 1.0, 0.0).astype(BF)
    permuted = dot(table[...], perm).astype(BF)
    place = lax.broadcasted_iota(jnp.int32, (N, BANDS), 0).astype(F32)
    for c in range(SLOTS):
        hit = (place == jnp.broadcast_to(starts + c, (N, BANDS))) & (
            jnp.broadcast_to(lens8[:1], (N, BANDS)) > c
        )
        one = jnp.where(hit, 1.0, 0.0).astype(BF)
        sel[c] = dot(permuted, one).astype(BF)
        sel_t[c] = lax.dot_general(
            one, permuted, (((0,), (1,)), ((), ())), preferred_element_type=F32
        ).astype(BF)
    first = QUART * g
    for c in range(SLOTS):

        def body(t, _):
            lane = pl.multiple_of(jnp.minimum(first + t, TILES - 1) * LANES, LANES)
            row = pl.multiple_of((c * QUART + t) * BANDS, BANDS)
            scr[pl.ds(row, BANDS), :] = stick[c, :, pl.ds(lane, LANES)].astype(F32)
            return 0

        lax.fori_loop(0, QUART, body, 0, unroll=True)

    b1 = lax.broadcasted_iota(jnp.int32, (16, BANDS), 1)
    r1 = lax.broadcasted_iota(jnp.int32, (16, BANDS), 0)
    pick = jnp.zeros((16, BANDS), F32)
    for k in range(SRC):
        pick = jnp.where((r1 == k) & (b1 == order_s[g * SRC + k]), 1.0, pick)
    pick = pick.astype(BF)
    for c in range(SLOTS):
        for u in range(TILES // 2):
            got = dot(pick, stick[c, :, u * 256 : u * 256 + 256])
            for h in range(2):
                for k in range(SRC):
                    flat = k * TILES + 2 * u + h
                    line = got[k : k + 1, h * LANES : (h + 1) * LANES]
                    if flat < WHOLE:
                        places = [(flat // EACH, flat % EACH)]
                    else:
                        places = [(8 * (flat - WHOLE) + i, EACH) for i in range(8)]
                    for d, r in places:
                        row = d * ROWS_S + c * SRC + r
                        scr_s[row : row + 1, :] = line

    def out_body(b, _):
        mine = scr[pl.ds(b, ROWS_T, stride=BANDS), :]
        tile = scr_s[pl.ds(pl.multiple_of(b * ROWS_S, 8), ROWS_S), :]
        msg[b] = jnp.concatenate([mine, tile], axis=0).astype(BF)
        return 0

    lax.fori_loop(0, BANDS, out_body, 0, unroll=8)


def rows_kernel(got, sel, quarter, piece, scr, last):
    def load(d, _):
        scr[pl.ds(pl.multiple_of(d * ROWS_M, 8), ROWS_M), :] = got[d].astype(F32)
        return 0

    lax.fori_loop(0, BANDS, load, 0, unroll=8)
    tables = [sel[c] for c in range(SLOTS)]

    def contracted(first, count, t):
        total = jnp.zeros((N, LANES), F32)
        for c in range(SLOTS):
            rows = scr[pl.ds(first + c * count + t, BANDS, stride=ROWS_M), :].astype(BF)
            total = total + dot(tables[c], rows)
        return total

    for r in range(EACH):
        piece[r * N : (r + 1) * N, :] = contracted(ROWS_T, SRC, r).astype(BF)
    last[:N, :] = contracted(ROWS_T, SRC, EACH)
    last[N:, :] = jnp.zeros((16, LANES), F32)
    band = lax.axis_index("band")
    piece[EACH * N :, :] = last[pl.ds((band & 7) * REST, 16), :].astype(BF)
    for t in range(QUART):
        quarter[t] = contracted(0, QUART, t).astype(BF)


def turned(scr, index):
    return jnp.concatenate(
        [
            scr[pl.ds(index, N, stride=PITCH), :].astype(BF),
            scr[pl.ds(index + 1, N, stride=PITCH), :].astype(BF),
        ],
        axis=1,
    )


def put(scr, index, values):
    scr[index * PITCH : index * PITCH + N, :] = values[:, :LANES]
    scr[(index + 1) * PITCH : (index + 1) * PITCH + N, :] = values[:, LANES:]


def side(ref, index):
    return jnp.concatenate([ref[index], ref[index + 1]], axis=1)


CHUNK = 5


def to_real(tile, out, table, expand, scr):
    for p in range(4):
        for lead in range(0, 10, CHUNK):
            rows = []
            for i in range(lead, lead + CHUNK):
                a = i * 5 + (160 * p) // LANES
                rows.append(jnp.concatenate([tile(a), tile(a + 1)], axis=1))
            res = dot(jnp.concatenate(rows, axis=0), expand[p])
            for j in range(CHUNK):
                put(scr, (lead + j) * 8 + 2 * p, res[j * N : (j + 1) * N])
    h = table[...]
    for x in range(0, N, 2):
        res = dot(h, turned(scr, x)).astype(BF)
        out[x] = res[:, :LANES]
        out[x + 1] = res[:, LANES:]


def target_kernel(own, got1, got2, got3, table, expand, out, scr, quarters):
    g = lax.axis_index("grp")
    for k, ref in enumerate((own, got1, got2, got3)):
        start = ((g - k) & 3) * QUART
        for t in range(QUART):
            quarters[start + t] = ref[t]
    to_real(lambda t: quarters[t], out, table, expand, scr)


def gather_tiles(groups, pieces, rest):
    band = lax.axis_index("band")
    core, z_at, x_at = band & 1, (band >> 1) & 7, band >> 4
    for ref, kx, flip, places in groups:
        for j, (back, swap) in enumerate(places):
            z = (z_at - back) & 7
            z = (z ^ 1) if swap else z
            origin = (((x_at - kx) & 3) * 8 + z) * 2 + (core ^ flip)
            whole = ref[j // 2, j % 2]
            for r in range(EACH):
                pieces[origin * EACH + r] = whole[r * N : (r + 1) * N]
            rest[pl.ds(origin * REST, REST), :] = whole[EACH * N :].astype(F32)[:REST]
    for j in range(SRC * TILES - WHOLE):
        pieces[WHOLE + j] = rest[j * N : (j + 1) * N, :].astype(BF)


def one_source(pieces, k, target, source, partial, table, expand, twin, screen, scr_a, scr_b):
    to_real(lambda t: pieces[k * TILES + t], source, table, expand, scr_a)
    h = table[...]
    turn = twin[...]
    for lead in range(0, N, 2 * CHUNK):
        rows = []
        for x in range(lead, lead + 2 * CHUNK, 2):
            rows.append(dot(h, side(target, x) * side(source, x)).astype(BF))
        res = dot(jnp.concatenate(rows, axis=0), turn)
        for j in range(CHUNK):
            put(scr_a, lead + 2 * j, res[j * N : (j + 1) * N])
    for y in range(0, N, 2):
        spec = dot(h, turned(scr_a, y))
        weight = jnp.concatenate([screen[min(y, N - y)], screen[min(y + 1, N - 1 - y)]], axis=1)
        put(scr_b, y, dot(h, (spec * weight).astype(BF)))
    for lead in range(0, N, 2 * CHUNK):
        rows = [turned(scr_b, x) for x in range(lead, lead + 2 * CHUNK, 2)]
        res = dot(jnp.concatenate(rows, axis=0), turn).astype(BF)
        for j in range(CHUNK):
            pot = dot(h, res[j * N : (j + 1) * N])
            for e in range(2):
                x = lead + 2 * j + e
                term = source[x].astype(F32) * pot[:, e * LANES : (e + 1) * LANES]
                partial[x] = partial[x] + term


def last_transform(partial, table, c0, c1, c2, scr, final):
    h = table[...]
    for x in range(0, N, 2):
        put(scr, x, dot(h, side(partial, x).astype(BF)))
    blocks = [[turned(scr, y + 2 * p) for p in range(4)] for y in range(0, N, 8)]
    for i in range(0, 10, CHUNK):
        eights = [jnp.concatenate(blocks[i + j], axis=1) for j in range(CHUNK)]
        r0 = dot(jnp.concatenate([v[:, :512] for v in eights], axis=0), c0[...]).astype(BF)
        r1 = dot(jnp.concatenate([v[:, 384:896] for v in eights], axis=0), c1[...]).astype(BF)
        r2 = dot(jnp.concatenate([v[:, 768:] for v in eights], axis=0), c2[...]).astype(BF)
        for j in range(CHUNK):
            t = (i + j) * 5
            rows = slice(j * N, (j + 1) * N)
            final[t] = r0[rows, :LANES]
            final[t + 1] = r0[rows, LANES:]
            final[t + 2] = r1[rows, :LANES]
            final[t + 3] = r1[rows, LANES:]
            final[t + 4] = r2[rows]
    final[TILES] = jnp.zeros((N, LANES), BF)
    final[TILES + 1] = jnp.zeros((N, LANES), BF)


def pairs_kernel(*refs):
    target, table, expand, twin, c0, c1, c2, screen = refs[10:18]
    outs = refs[18:22]
    source, partial, scr_a, scr_b, final, pieces, rest = refs[22:]
    g = lax.axis_index("grp")
    places = [(back, swap) for back in (0, 2, 4, 6) for swap in (False, True)]
    groups = []
    for flip in range(2):
        own, ahead, behind, far_a, far_b = refs[5 * flip : 5 * flip + 5]
        groups += [(own, 0, flip, places), (ahead, 1, flip, places), (behind, 3, flip, places)]
        groups += [(far_a, 2, flip, places[:4]), (far_b, 2, flip, places[4:])]
    gather_tiles(groups, pieces, rest)
    partial[...] = jnp.zeros_like(partial)

    def body(k, _):
        one_source(pieces, k, target, source, partial, table, expand, twin, screen, scr_a, scr_b)
        return 0

    lax.fori_loop(0, SRC, body, 0)
    last_transform(partial, table, c0, c1, c2, scr_a, final)
    for k, out in enumerate(outs):
        start = ((g + k) & 3) * QUART
        for t in range(QUART):
            out[t] = final[start + t]


def select_kernel(own, got1, got2, got3, sel_t, msg, scr):
    tables = [sel_t[c] for c in range(SLOTS)]
    for t in range(QUART):
        total = (
            own[t].astype(F32) + got1[t].astype(F32) + got2[t].astype(F32) + got3[t].astype(F32)
        ).astype(BF)
        for c in range(SLOTS):
            scr[(c * QUART + t) * BANDS : (c * QUART + t + 1) * BANDS, :] = dot(tables[c], total)

    def body(d, _):
        msg[d] = scr[pl.ds(d, ROWS_T, stride=BANDS), :].astype(BF)
        return 0

    lax.fori_loop(0, BANDS, body, 0, unroll=8)


def rows_out_kernel(got, low, high, scr):
    def load(b, _):
        scr[pl.ds(pl.multiple_of(b * ROWS_T, 8), ROWS_T), :] = got[b].astype(F32)
        return 0

    lax.fori_loop(0, BANDS, load, 0, unroll=8)
    for c in range(SLOTS):
        for t in range(QUART):
            rows = scr[pl.ds(c * QUART + t, BANDS, stride=ROWS_T), :].astype(BF)
            low[c, :, t * LANES : (t + 1) * LANES] = rows[:HALF]
            high[c, :, t * LANES : (t + 1) * LANES] = rows[HALF:]


def join_kernel(*refs):
    out = refs[8]
    g = lax.axis_index("grp")
    wide = QUART * LANES
    short = (TILES - 3 * QUART) * LANES
    for k in range(4):
        origin = (g - k) & 3
        start = pl.multiple_of(origin * wide, LANES)

        @pl.when(origin < 3)
        def _():
            for c in range(SLOTS):
                for e in range(2):
                    out[c, e * HALF : (e + 1) * HALF, pl.ds(start, wide)] = refs[2 * k + e][c]

        @pl.when(origin == 3)
        def _():
            for c in range(SLOTS):
                for e in range(2):
                    out[c, e * HALF : (e + 1) * HALF, 3 * wide :] = refs[2 * k + e][c, :, :short]


VM = pl.BlockSpec(memory_space=pltpu.VMEM)
SM = pl.BlockSpec(memory_space=pltpu.SMEM)
ANY = pl.BlockSpec(memory_space=pl.ANY)
PARAMS = pltpu.CompilerParams(vmem_limit_bytes=56 * 1024 * 1024)


def shape(dims, kind=BF):
    return jax.ShapeDtypeStruct(dims, kind)


def shift_grp(value, k):
    return lax.ppermute(value, "grp", [(i, (i + k) % GROUPS) for i in range(GROUPS)])


def swap_band(value, axis):
    bit = {"core": 1, "z": 2}[axis]
    return lax.ppermute(value, "band", [(i, i ^ bit) for i in range(BANDS)])


def shift_band(value, dx, dz, dc):
    moves = []
    for x in range(4):
        for z in range(8):
            for c in range(2):
                there = (((x + dx) % 4) * 8 + (z + dz) % 8) * 2 + (c + dc) % 2
                moves.append(((x * 8 + z) * 2 + c, there))
    return lax.ppermute(value, "band", moves)


def ring_gather(first, second, step):
    ahead = step(first, 1), step(second, 1)
    behind = step(first, 3), step(second, 3)
    far = step(ahead[0], 1), step(behind[1], 3)
    return [(first, second), ahead, far, behind]


def shards(stick_data, row_lengths, row_order, source_order):
    table = jnp.asarray(hartley_table())
    expand = jnp.asarray(expand_tables(hartley_table()))
    twin = jnp.asarray(pair_table(hartley_table()))
    c0, c1, c2 = (jnp.asarray(v) for v in compress_tables(hartley_table()))
    screen = jnp.asarray(screen_table())

    msg, sel, sel_t = pl.pallas_call(
        pack_kernel,
        out_shape=(
            shape((BANDS, ROWS_M, LANES)),
            shape((SLOTS, N, BANDS)),
            shape((SLOTS, BANDS, N)),
        ),
        in_specs=[SM, VM, VM, VM, VM],
        out_specs=(VM, VM, VM),
        scratch_shapes=[
            pltpu.VMEM((ROWS_T * BANDS, LANES), F32),
            pltpu.VMEM((BANDS * ROWS_S, LANES), F32),
        ],
        compiler_params=PARAMS,
    )(source_order, stick_data, row_lengths.reshape(1, BANDS), row_order.reshape(1, N), table)
    got = lax.all_to_all(msg, "band", 0, 0, tiled=True)
    quarter, piece = pl.pallas_call(
        rows_kernel,
        out_shape=(shape((QUART, N, LANES)), shape((PIECE, LANES))),
        in_specs=[VM, VM],
        out_specs=(VM, VM),
        scratch_shapes=[
            pltpu.VMEM((ROWS_M * BANDS, LANES), F32),
            pltpu.VMEM((N + 16, LANES), F32),
        ],
        compiler_params=PARAMS,
    )(got, sel)

    swapped = swap_band(piece, "z")
    quarters = [quarter] + [shift_grp(quarter, k) for k in range(1, 4)]
    couple = jnp.stack([piece, swapped])
    along_z = jnp.stack([couple] + [shift_band(couple, 0, k, 0) for k in (2, 4, 6)])

    target = pl.pallas_call(
        target_kernel,
        out_shape=shape((N, N, LANES)),
        in_specs=[VM] * 6,
        out_specs=VM,
        scratch_shapes=[
            pltpu.VMEM((N * PITCH, LANES), F32),
            pltpu.VMEM((4 * QUART, N, LANES), BF),
        ],
        compiler_params=PARAMS,
    )(*quarters, table, expand)

    along_z, target = lax.optimization_barrier((along_z, target))
    ahead, behind = shift_band(along_z, 1, 0, 0), shift_band(along_z, 3, 0, 0)
    far_a, far_b = shift_band(ahead[:2], 1, 0, 0), shift_band(behind[2:], 3, 0, 0)
    same_core = [along_z, ahead, behind, far_a, far_b]
    other_core = [shift_band(v, 0, 0, 1) for v in same_core]

    outs = pl.pallas_call(
        pairs_kernel,
        out_shape=tuple(shape((QUART, N, LANES)) for _ in range(4)),
        in_specs=[VM] * 18,
        out_specs=(VM,) * 4,
        scratch_shapes=[
            pltpu.VMEM((N, N, LANES), BF),
            pltpu.VMEM((N, N, LANES), F32),
            pltpu.VMEM((N * PITCH, LANES), F32),
            pltpu.VMEM((N * PITCH, LANES), F32),
            pltpu.VMEM((TILES + 2, N, LANES), BF),
            pltpu.VMEM((SRC * TILES, N, LANES), BF),
            pltpu.VMEM((BANDS * REST, LANES), F32),
        ],
        compiler_params=PARAMS,
    )(*same_core, *other_core, target, table, expand, twin, c0, c1, c2, screen)

    parts = [outs[0]] + [shift_grp(outs[k], k) for k in range(1, 4)]
    message = pl.pallas_call(
        select_kernel,
        out_shape=shape((BANDS, ROWS_T, LANES)),
        in_specs=[VM] * 5,
        out_specs=VM,
        scratch_shapes=[pltpu.VMEM((ROWS_T * BANDS, LANES), F32)],
        compiler_params=PARAMS,
    )(*parts, sel_t)

    received = lax.all_to_all(message, "band", 0, 0, tiled=True)
    low, high = pl.pallas_call(
        rows_out_kernel,
        out_shape=(shape((SLOTS, HALF, QUART * LANES)),) * 2,
        in_specs=[VM],
        out_specs=(VM, VM),
        scratch_shapes=[pltpu.VMEM((ROWS_T * BANDS, LANES), F32)],
        compiler_params=PARAMS,
    )(received)

    spread = ring_gather(low, high, shift_grp)
    return pl.pallas_call(
        join_kernel,
        out_shape=shape((SLOTS, BANDS, TILES * LANES)),
        in_specs=[VM] * 8,
        out_specs=VM,
        compiler_params=PARAMS,
    )(*[v for both in spread for v in both])


def solution(mesh):
    return jax.shard_map(
        shards,
        mesh=mesh,
        in_specs=(P("band", None, None), P(), P(), P()),
        out_specs=P("band", None, None),
        check_vma=False,
    )
```

```python
import functools
import math

import jax
import jax.numpy as jnp
import numpy as np
from jax import lax
from jax.experimental import pallas as pl
from jax.experimental.pallas import tpu as pltpu
from jax.sharding import PartitionSpec as P

N = 80
LANES = 128
TILES = 50
QUART = 13
SRC = 4
SLOTS = 3
BANDS = 64
GROUPS = 4
ROWS_T = 40
ROWS_S = 16
EACH = 3
SLAB = 16
WHOLE = EACH * SLAB
REST = 10
PIECE = 256
ROWS_M = ROWS_T + ROWS_S
HALF = BANDS // 2
PITCH = 88
BF = jnp.bfloat16
F32 = jnp.float32

coulomb_peak = 4.0
screen_square = 64.0


def hartley_table():
    index = np.arange(N)
    angles = (index[:, None] * index[None, :] % N).astype(np.float32) * np.float32(2.0 * math.pi / N)
    return ((np.cos(angles) + np.sin(angles)) / np.float32(math.sqrt(N))).astype(BF)


def expand_tables(table):
    out = np.zeros((4, 256, 256), BF)
    for p in range(4):
        off = 160 * p % LANES
        out[p, off : off + N, :N] = table
        out[p, off + N : off + 2 * N, LANES : LANES + N] = table
    return out


def pair_table(table):
    out = np.zeros((256, 256), BF)
    out[:N, :N] = table
    out[LANES : LANES + N, LANES : LANES + N] = table
    return out


def compress_tables(table):
    whole = np.zeros((1024, 640), BF)
    for y in range(8):
        whole[y * LANES : y * LANES + N, y * N : (y + 1) * N] = table
    return whole[:512, :256].copy(), whole[384:896, 256:512].copy(), whole[768:, 512:].copy()


def screen_table():
    freq = np.minimum(np.arange(N), N - np.arange(N)).astype(np.float32)
    sq = freq * freq
    total = sq[:41, None, None] + sq[None, :, None] + sq[None, None, :]
    out = np.zeros((41, N, LANES), np.float32)
    out[:, :, :N] = np.float32(coulomb_peak) / (np.float32(1.0) + total / np.float32(screen_square))
    return out


def dot(a, b):
    return jnp.dot(a, b, preferred_element_type=F32)


def dot_tn(a, b):
    return lax.dot_general(a, b, (((0,), (0,)), ((), ())), preferred_element_type=F32)


def pack_kernel(order_s, stick, lengths, order_v, table, msg, sel, sel_t, scr, scr_s):
    g = lax.axis_index("grp")
    lens = lengths[...]
    d0 = lax.broadcasted_iota(jnp.int32, (BANDS, BANDS), 0)
    d1 = lax.broadcasted_iota(jnp.int32, (BANDS, BANDS), 1)
    before = jnp.where(d0 < d1, 1.0, 0.0).astype(BF)
    lens8 = jnp.broadcast_to(lens, (8, BANDS)).astype(F32)
    starts = dot(lens8.astype(BF), before)[:1]
    q0 = lax.broadcasted_iota(jnp.int32, (N, N), 0)
    perm = jnp.where(jnp.broadcast_to(order_v[...], (N, N)) == q0, 1.0, 0.0).astype(BF)
    permuted = dot(table[...], perm).astype(BF)
    place = lax.broadcasted_iota(jnp.int32, (N, BANDS), 0).astype(F32)
    for c in range(SLOTS):
        hit = (place == jnp.broadcast_to(starts + c, (N, BANDS))) & (
            jnp.broadcast_to(lens8[:1], (N, BANDS)) > c
        )
        one = jnp.where(hit, 1.0, 0.0).astype(BF)
        sel[c] = dot(permuted, one).astype(BF)
        sel_t[c] = lax.dot_general(
            one, permuted, (((0,), (1,)), ((), ())), preferred_element_type=F32
        ).astype(BF)
    first = QUART * g
    for c in range(SLOTS):

        def body(t, _):
            lane = pl.multiple_of(jnp.minimum(first + t, TILES - 1) * LANES, LANES)
            row = pl.multiple_of((c * QUART + t) * BANDS, BANDS)
            scr[pl.ds(row, BANDS), :] = stick[c, :, pl.ds(lane, LANES)].astype(F32)
            return 0

        lax.fori_loop(0, QUART, body, 0, unroll=True)

    b1 = lax.broadcasted_iota(jnp.int32, (16, BANDS), 1)
    r1 = lax.broadcasted_iota(jnp.int32, (16, BANDS), 0)
    pick = jnp.zeros((16, BANDS), F32)
    for k in range(SRC):
        pick = jnp.where((r1 == k) & (b1 == order_s[g * SRC + k]), 1.0, pick)
    pick = pick.astype(BF)
    for c in range(SLOTS):
        for u in range(TILES // 2):
            got = dot(pick, stick[c, :, u * 256 : u * 256 + 256])
            for h in range(2):
                for k in range(SRC):
                    t = 2 * u + h
                    line = got[k : k + 1, h * LANES : (h + 1) * LANES]
                    if t < WHOLE:
                        places = [(t // EACH, t % EACH)]
                    else:
                        places = [(8 * (t - WHOLE) + i, EACH) for i in range(8)]
                    for d, r in places:
                        row = (k * SLAB + d) * ROWS_S + c * SRC + r
                        scr_s[row : row + 1, :] = line

    def out_body(b, _):
        mine = scr[pl.ds(b, ROWS_T, stride=BANDS), :]
        tile = scr_s[pl.ds(pl.multiple_of(b * ROWS_S, 8), ROWS_S), :]
        msg[b] = jnp.concatenate([mine, tile], axis=0).astype(BF)
        return 0

    lax.fori_loop(0, BANDS, out_body, 0, unroll=8)


def rows_kernel(got, sel, quarter, piece, scr, last):
    def load(d, _):
        scr[pl.ds(pl.multiple_of(d * ROWS_M, 8), ROWS_M), :] = got[d].astype(F32)
        return 0

    lax.fori_loop(0, BANDS, load, 0, unroll=8)
    tables = [sel[c] for c in range(SLOTS)]

    def contracted(first, count, t):
        total = jnp.zeros((N, LANES), F32)
        for c in range(SLOTS):
            rows = scr[pl.ds(first + c * count + t, BANDS, stride=ROWS_M), :].astype(BF)
            total = total + dot(tables[c], rows)
        return total

    for r in range(EACH):
        piece[r * N : (r + 1) * N, :] = contracted(ROWS_T, SRC, r).astype(BF)
    last[:N, :] = contracted(ROWS_T, SRC, EACH)
    last[N:, :] = jnp.zeros((16, LANES), F32)
    band = lax.axis_index("band")
    piece[EACH * N :, :] = last[pl.ds((band & 7) * REST, 16), :].astype(BF)
    for t in range(QUART):
        quarter[t] = contracted(0, QUART, t).astype(BF)


def turned(scr, index):
    return jnp.concatenate(
        [
            scr[pl.ds(index, N, stride=PITCH), :].astype(BF),
            scr[pl.ds(index + 1, N, stride=PITCH), :].astype(BF),
        ],
        axis=1,
    )


def put(scr, index, values):
    scr[index * PITCH : index * PITCH + N, :] = values[:, :LANES]
    scr[(index + 1) * PITCH : (index + 1) * PITCH + N, :] = values[:, LANES:]


def side(ref, index):
    return jnp.concatenate([ref[index], ref[index + 1]], axis=1)


CHUNK = 5


def to_real(tile, out, table, expand, scr):
    for p in range(4):
        for lead in range(0, 10, CHUNK):
            rows = []
            for i in range(lead, lead + CHUNK):
                a = i * 5 + (160 * p) // LANES
                rows.append(jnp.concatenate([tile(a), tile(a + 1)], axis=1))
            res = dot(jnp.concatenate(rows, axis=0), expand[p])
            for j in range(CHUNK):
                put(scr, (lead + j) * 8 + 2 * p, res[j * N : (j + 1) * N])
    h = table[...]
    for x in range(0, N, 2):
        res = dot(h, turned(scr, x)).astype(BF)
        out[x] = res[:, :LANES]
        out[x + 1] = res[:, LANES:]


def target_kernel(own, got1, got2, got3, table, expand, out, scr, quarters):
    g = lax.axis_index("grp")
    for k, ref in enumerate((own, got1, got2, got3)):
        start = ((g - k) & 3) * QUART
        for t in range(QUART):
            quarters[start + t] = ref[t]
    to_real(lambda t: quarters[t], out, table, expand, scr)


PLACES = [(back, swap) for back in (0, 2, 4, 6) for swap in (False, True)]


def gather_tiles(same, other, pieces, lead, rest):
    band = lax.axis_index("band")
    core, z_at = band & 1, (band >> 1) & 7
    for refs, flip in ((same, 0), (other, 1)):
        couples = [ref.at[i] for ref in refs for i in range(ref.shape[0])]
        for j, (back, swap) in enumerate(PLACES):
            z = (z_at - back) & 7
            z = (z ^ 1) if swap else z
            origin = z * 2 + (core ^ flip)
            whole = couples[j // 2][j % 2]
            for r in range(EACH):
                pieces[lead + origin * EACH + r] = whole[r * N : (r + 1) * N]
            rest[pl.ds(origin * REST, REST), :] = whole[EACH * N :].astype(F32)[:REST]
    for j in range(TILES - WHOLE):
        pieces[lead + WHOLE + j] = rest[j * N : (j + 1) * N, :].astype(BF)


def one_source(pieces, k, target, source, before, partial, table, expand, twin, screen, scr_a, scr_b):
    to_real(lambda t: pieces[k * TILES + t], source, table, expand, scr_a)
    h = table[...]
    turn = twin[...]
    for lead in range(0, N, 2 * CHUNK):
        rows = []
        for x in range(lead, lead + 2 * CHUNK, 2):
            rows.append(dot(h, side(target, x) * side(source, x)).astype(BF))
        res = dot(jnp.concatenate(rows, axis=0), turn)
        for j in range(CHUNK):
            put(scr_a, lead + 2 * j, res[j * N : (j + 1) * N])
    for y in range(0, N, 2):
        spec = dot(h, turned(scr_a, y))
        weight = jnp.concatenate([screen[min(y, N - y)], screen[min(y + 1, N - 1 - y)]], axis=1)
        put(scr_b, y, dot(h, (spec * weight).astype(BF)))
    for lead in range(0, N, 2 * CHUNK):
        rows = [turned(scr_b, x) for x in range(lead, lead + 2 * CHUNK, 2)]
        res = dot(jnp.concatenate(rows, axis=0), turn).astype(BF)
        for j in range(CHUNK):
            pot = dot(h, res[j * N : (j + 1) * N])
            for e in range(2):
                x = lead + 2 * j + e
                term = source[x].astype(F32) * pot[:, e * LANES : (e + 1) * LANES]
                partial[x] = term if before is None else before[x] + term


def last_transform(partial, table, c0, c1, c2, scr, final):
    h = table[...]
    for x in range(0, N, 2):
        put(scr, x, dot(h, side(partial, x).astype(BF)))
    blocks = [[turned(scr, y + 2 * p) for p in range(4)] for y in range(0, N, 8)]
    for i in range(0, 10, CHUNK):
        eights = [jnp.concatenate(blocks[i + j], axis=1) for j in range(CHUNK)]
        r0 = dot(jnp.concatenate([v[:, :512] for v in eights], axis=0), c0[...]).astype(BF)
        r1 = dot(jnp.concatenate([v[:, 384:896] for v in eights], axis=0), c1[...]).astype(BF)
        r2 = dot(jnp.concatenate([v[:, 768:] for v in eights], axis=0), c2[...]).astype(BF)
        for j in range(CHUNK):
            t = (i + j) * 5
            rows = slice(j * N, (j + 1) * N)
            final[t] = r0[rows, :LANES]
            final[t + 1] = r0[rows, LANES:]
            final[t + 2] = r1[rows, :LANES]
            final[t + 3] = r1[rows, LANES:]
            final[t + 4] = r2[rows]
    final[TILES] = jnp.zeros((N, LANES), BF)
    final[TILES + 1] = jnp.zeros((N, LANES), BF)


def pairs_kernel(kinds, first, last, *refs):
    refs = list(refs)
    take = lambda n: [refs.pop(0) for _ in range(n)]
    sources = [(take(n), take(n)) for n in kinds]
    target, table, expand, twin, screen = take(5)
    before = None if first else take(1)[0]
    tables = take(3) if last else []
    outs = take(4) if last else take(1)
    source, scr_a, scr_b, pieces, rest = take(5)
    partial, final = take(2) if last else (outs[0], None)
    for i, (same, other) in enumerate(sources):
        gather_tiles(same, other, pieces, i * TILES, rest)
    work = (table, expand, twin, screen, scr_a, scr_b)
    if len(kinds) == 1:
        one_source(pieces, 0, target, source, before, partial, *work)
    else:
        partial[...] = before[...]

        def body(k, _):
            one_source(pieces, k, target, source, partial, partial, *work)
            return 0

        lax.fori_loop(0, len(kinds), body, 0)
    if last:
        last_transform(partial, table, *tables, scr_a, final)
        g = lax.axis_index("grp")
        for k, out in enumerate(outs):
            start = ((g + k) & 3) * QUART
            for t in range(QUART):
                out[t] = final[start + t]


def call_pairs(sources, target, tables, before=None, ends=None):
    kinds = tuple(len(same) for same, _ in sources)
    last = ends is not None
    operands = [v for same, other in sources for v in list(same) + list(other)]
    operands += [target, *tables] + ([] if before is None else [before]) + list(ends or [])
    scratch = [
        pltpu.VMEM((N, N, LANES), BF),
        pltpu.VMEM((N * PITCH, LANES), F32),
        pltpu.VMEM((N * PITCH, LANES), F32),
        pltpu.VMEM((len(kinds) * TILES, N, LANES), BF),
        pltpu.VMEM((SLAB * REST, LANES), F32),
    ]
    if last:
        scratch += [pltpu.VMEM((N, N, LANES), F32), pltpu.VMEM((TILES + 2, N, LANES), BF)]
    return pl.pallas_call(
        functools.partial(pairs_kernel, kinds, before is None, last),
        out_shape=tuple(shape((QUART, N, LANES)) for _ in range(4)) if last else shape((N, N, LANES), F32),
        in_specs=[VM] * len(operands),
        out_specs=(VM,) * 4 if last else VM,
        scratch_shapes=scratch,
        compiler_params=LARGE,
        cost_estimate=pl.CostEstimate(
            flops=6_000_000_000 * len(kinds), bytes_accessed=8_000_000, transcendentals=0
        ),
    )(*operands)


def select_kernel(own, got1, got2, got3, sel_t, msg, scr):
    tables = [sel_t[c] for c in range(SLOTS)]
    for t in range(QUART):
        total = (
            own[t].astype(F32) + got1[t].astype(F32) + got2[t].astype(F32) + got3[t].astype(F32)
        ).astype(BF)
        for c in range(SLOTS):
            scr[(c * QUART + t) * BANDS : (c * QUART + t + 1) * BANDS, :] = dot(tables[c], total)

    def body(d, _):
        msg[d] = scr[pl.ds(d, ROWS_T, stride=BANDS), :].astype(BF)
        return 0

    lax.fori_loop(0, BANDS, body, 0, unroll=8)


def rows_out_kernel(got, low, high, scr):
    def load(b, _):
        scr[pl.ds(pl.multiple_of(b * ROWS_T, 8), ROWS_T), :] = got[b].astype(F32)
        return 0

    lax.fori_loop(0, BANDS, load, 0, unroll=8)
    for c in range(SLOTS):
        for t in range(QUART):
            rows = scr[pl.ds(c * QUART + t, BANDS, stride=ROWS_T), :].astype(BF)
            low[c, :, t * LANES : (t + 1) * LANES] = rows[:HALF]
            high[c, :, t * LANES : (t + 1) * LANES] = rows[HALF:]


def join_kernel(*refs):
    out = refs[8]
    g = lax.axis_index("grp")
    wide = QUART * LANES
    short = (TILES - 3 * QUART) * LANES
    for k in range(4):
        origin = (g - k) & 3
        start = pl.multiple_of(origin * wide, LANES)

        @pl.when(origin < 3)
        def _():
            for c in range(SLOTS):
                for e in range(2):
                    out[c, e * HALF : (e + 1) * HALF, pl.ds(start, wide)] = refs[2 * k + e][c]

        @pl.when(origin == 3)
        def _():
            for c in range(SLOTS):
                for e in range(2):
                    out[c, e * HALF : (e + 1) * HALF, 3 * wide :] = refs[2 * k + e][c, :, :short]


VM = pl.BlockSpec(memory_space=pltpu.VMEM)
SM = pl.BlockSpec(memory_space=pltpu.SMEM)
ANY = pl.BlockSpec(memory_space=pl.ANY)
PARAMS = pltpu.CompilerParams(vmem_limit_bytes=16 * 1024 * 1024)
LARGE = pltpu.CompilerParams(vmem_limit_bytes=30 * 1024 * 1024)


def shape(dims, kind=BF):
    return jax.ShapeDtypeStruct(dims, kind)


def shift_grp(value, k):
    return lax.ppermute(value, "grp", [(i, (i + k) % GROUPS) for i in range(GROUPS)])


def swap_band(value, axis):
    bit = {"core": 1, "z": 2}[axis]
    return lax.ppermute(value, "band", [(i, i ^ bit) for i in range(BANDS)])


def shift_band(value, dx, dz, dc):
    moves = []
    for x in range(4):
        for z in range(8):
            for c in range(2):
                there = (((x + dx) % 4) * 8 + (z + dz) % 8) * 2 + (c + dc) % 2
                moves.append(((x * 8 + z) * 2 + c, there))
    return lax.ppermute(value, "band", moves)


def ring_gather(first, second, step):
    ahead = step(first, 1), step(second, 1)
    behind = step(first, 3), step(second, 3)
    far = step(ahead[0], 1), step(behind[1], 3)
    return [(first, second), ahead, far, behind]


def shards(stick_data, row_lengths, row_order, source_order):
    table = jnp.asarray(hartley_table())
    expand = jnp.asarray(expand_tables(hartley_table()))
    twin = jnp.asarray(pair_table(hartley_table()))
    c0, c1, c2 = (jnp.asarray(v) for v in compress_tables(hartley_table()))
    screen = jnp.asarray(screen_table())

    msg, sel, sel_t = pl.pallas_call(
        pack_kernel,
        out_shape=(
            shape((BANDS, ROWS_M, LANES)),
            shape((SLOTS, N, BANDS)),
            shape((SLOTS, BANDS, N)),
        ),
        in_specs=[SM, VM, VM, VM, VM],
        out_specs=(VM, VM, VM),
        scratch_shapes=[
            pltpu.VMEM((ROWS_T * BANDS, LANES), F32),
            pltpu.VMEM((BANDS * ROWS_S, LANES), F32),
        ],
        compiler_params=PARAMS,
    )(source_order, stick_data, row_lengths.reshape(1, BANDS), row_order.reshape(1, N), table)
    got = lax.all_to_all(msg, "band", 0, 0, tiled=True)
    quarter, piece = pl.pallas_call(
        rows_kernel,
        out_shape=(shape((QUART, N, LANES)), shape((PIECE, LANES))),
        in_specs=[VM, VM],
        out_specs=(VM, VM),
        scratch_shapes=[
            pltpu.VMEM((ROWS_M * BANDS, LANES), F32),
            pltpu.VMEM((N + 16, LANES), F32),
        ],
        compiler_params=PARAMS,
    )(got, sel)

    swapped = swap_band(piece, "z")
    quarters = [quarter] + [shift_grp(quarter, k) for k in range(1, 4)]
    couple = jnp.stack([piece, swapped])
    along_z = jnp.stack([couple] + [shift_band(couple, 0, k, 0) for k in (2, 4, 6)])

    along_z, *quarters = lax.optimization_barrier((along_z, *quarters))
    target = pl.pallas_call(
        target_kernel,
        out_shape=shape((N, N, LANES)),
        in_specs=[VM] * 6,
        out_specs=VM,
        scratch_shapes=[
            pltpu.VMEM((N * PITCH, LANES), F32),
            pltpu.VMEM((4 * QUART, N, LANES), BF),
        ],
        compiler_params=PARAMS,
    )(*quarters, table, expand)

    ahead, behind = shift_band(along_z, 1, 0, 0), shift_band(along_z, 3, 0, 0)
    far = shift_band(ahead[:2], 1, 0, 0), shift_band(behind[2:], 3, 0, 0)
    flip = lambda v: shift_band(v, 0, 0, 1)

    tables = (table, expand, twin, screen)
    partial = call_pairs([([along_z], [flip(along_z)])], target, tables)
    partial = call_pairs(
        [([v], [flip(v)]) for v in (ahead, behind)], target, tables, before=partial
    )
    outs = call_pairs(
        [(far, [flip(v) for v in far])], target, tables, before=partial, ends=(c0, c1, c2)
    )

    parts = [outs[0]] + [shift_grp(outs[k], k) for k in range(1, 4)]
    message = pl.pallas_call(
        select_kernel,
        out_shape=shape((BANDS, ROWS_T, LANES)),
        in_specs=[VM] * 5,
        out_specs=VM,
        scratch_shapes=[pltpu.VMEM((ROWS_T * BANDS, LANES), F32)],
        compiler_params=PARAMS,
    )(*parts, sel_t)

    received = lax.all_to_all(message, "band", 0, 0, tiled=True)
    low, high = pl.pallas_call(
        rows_out_kernel,
        out_shape=(shape((SLOTS, HALF, QUART * LANES)),) * 2,
        in_specs=[VM],
        out_specs=(VM, VM),
        scratch_shapes=[pltpu.VMEM((ROWS_T * BANDS, LANES), F32)],
        compiler_params=PARAMS,
    )(received)

    spread = ring_gather(low, high, shift_grp)
    return pl.pallas_call(
        join_kernel,
        out_shape=shape((SLOTS, BANDS, TILES * LANES)),
        in_specs=[VM] * 8,
        out_specs=VM,
        compiler_params=PARAMS,
    )(*[v for both in spread for v in both])


def solution(mesh):
    return jax.shard_map(
        shards,
        mesh=mesh,
        in_specs=(P("band", None, None), P(), P(), P()),
        out_specs=P("band", None, None),
        check_vma=False,
    )
```

```python
import functools
import math

import jax
import jax.numpy as jnp
import numpy as np
from jax import lax
from jax.experimental import pallas as pl
from jax.experimental.pallas import tpu as pltpu
from jax.sharding import PartitionSpec as P

N = 80
LANES = 128
TILES = 50
QUART = 13
SRC = 4
SLOTS = 3
BANDS = 64
GROUPS = 4
ROWS_T = 40
ROWS_S = 16
EACH = 3
SLAB = 16
WHOLE = EACH * SLAB
REST = 10
PIECE = 256
ROWS_M = ROWS_T + ROWS_S
HALF = BANDS // 2
PITCH = 88
BF = jnp.bfloat16
F32 = jnp.float32

coulomb_peak = 4.0
screen_square = 64.0


def hartley_table():
    index = np.arange(N)
    angles = (index[:, None] * index[None, :] % N).astype(np.float32) * np.float32(2.0 * math.pi / N)
    return ((np.cos(angles) + np.sin(angles)) / np.float32(math.sqrt(N))).astype(BF)


def expand_tables(table):
    out = np.zeros((4, 256, 256), BF)
    for p in range(4):
        off = 160 * p % LANES
        out[p, off : off + N, :N] = table
        out[p, off + N : off + 2 * N, LANES : LANES + N] = table
    return out


def pair_table(table):
    out = np.zeros((256, 256), BF)
    out[:N, :N] = table
    out[LANES : LANES + N, LANES : LANES + N] = table
    return out


def compress_tables(table):
    whole = np.zeros((1024, 640), BF)
    for y in range(8):
        whole[y * LANES : y * LANES + N, y * N : (y + 1) * N] = table
    return whole[:512, :256].copy(), whole[384:896, 256:512].copy(), whole[768:, 512:].copy()


def screen_table():
    freq = np.minimum(np.arange(N), N - np.arange(N)).astype(np.float32)
    sq = freq * freq
    total = sq[:41, None, None] + sq[None, :, None] + sq[None, None, :]
    out = np.zeros((41, N, LANES), np.float32)
    out[:, :, :N] = np.float32(coulomb_peak) / (np.float32(1.0) + total / np.float32(screen_square))
    return out


def dot(a, b):
    return jnp.dot(a, b, preferred_element_type=F32)


def dot_tn(a, b):
    return lax.dot_general(a, b, (((0,), (0,)), ((), ())), preferred_element_type=F32)


def pack_kernel(order_s, stick, lengths, order_v, table, msg, sel, sel_t, scr, scr_s):
    g = lax.axis_index("grp")
    lens = lengths[...]
    d0 = lax.broadcasted_iota(jnp.int32, (BANDS, BANDS), 0)
    d1 = lax.broadcasted_iota(jnp.int32, (BANDS, BANDS), 1)
    before = jnp.where(d0 < d1, 1.0, 0.0).astype(BF)
    lens8 = jnp.broadcast_to(lens, (8, BANDS)).astype(F32)
    starts = dot(lens8.astype(BF), before)[:1]
    q0 = lax.broadcasted_iota(jnp.int32, (N, N), 0)
    perm = jnp.where(jnp.broadcast_to(order_v[...], (N, N)) == q0, 1.0, 0.0).astype(BF)
    permuted = dot(table[...], perm).astype(BF)
    place = lax.broadcasted_iota(jnp.int32, (N, BANDS), 0).astype(F32)
    for c in range(SLOTS):
        hit = (place == jnp.broadcast_to(starts + c, (N, BANDS))) & (
            jnp.broadcast_to(lens8[:1], (N, BANDS)) > c
        )
        one = jnp.where(hit, 1.0, 0.0).astype(BF)
        sel[c] = dot(permuted, one).astype(BF)
        sel_t[c] = lax.dot_general(
            one, permuted, (((0,), (1,)), ((), ())), preferred_element_type=F32
        ).astype(BF)
    first = QUART * g
    for c in range(SLOTS):

        def body(t, _):
            lane = pl.multiple_of(jnp.minimum(first + t, TILES - 1) * LANES, LANES)
            row = pl.multiple_of((c * QUART + t) * BANDS, BANDS)
            scr[pl.ds(row, BANDS), :] = stick[c, :, pl.ds(lane, LANES)].astype(F32)
            return 0

        lax.fori_loop(0, QUART, body, 0, unroll=True)

    b1 = lax.broadcasted_iota(jnp.int32, (16, BANDS), 1)
    r1 = lax.broadcasted_iota(jnp.int32, (16, BANDS), 0)
    pick = jnp.zeros((16, BANDS), F32)
    for k in range(SRC):
        pick = jnp.where((r1 == k) & (b1 == order_s[g * SRC + k]), 1.0, pick)
    pick = pick.astype(BF)
    for c in range(SLOTS):
        for u in range(TILES // 2):
            got = dot(pick, stick[c, :, u * 256 : u * 256 + 256])
            for h in range(2):
                for k in range(SRC):
                    t = 2 * u + h
                    line = got[k : k + 1, h * LANES : (h + 1) * LANES]
                    if t < WHOLE:
                        places = [(t // EACH, t % EACH)]
                    else:
                        places = [(8 * (t - WHOLE) + i, EACH) for i in range(8)]
                    for d, r in places:
                        row = (k * SLAB + d) * ROWS_S + c * SRC + r
                        scr_s[row : row + 1, :] = line

    def out_body(b, _):
        mine = scr[pl.ds(b, ROWS_T, stride=BANDS), :]
        tile = scr_s[pl.ds(pl.multiple_of(b * ROWS_S, 8), ROWS_S), :]
        msg[b] = jnp.concatenate([mine, tile], axis=0).astype(BF)
        return 0

    lax.fori_loop(0, BANDS, out_body, 0, unroll=8)


def rows_kernel(got, sel, quarter, piece, scr, last):
    def load(d, _):
        scr[pl.ds(pl.multiple_of(d * ROWS_M, 8), ROWS_M), :] = got[d].astype(F32)
        return 0

    lax.fori_loop(0, BANDS, load, 0, unroll=8)
    tables = [sel[c] for c in range(SLOTS)]

    def contracted(first, count, t):
        total = jnp.zeros((N, LANES), F32)
        for c in range(SLOTS):
            rows = scr[pl.ds(first + c * count + t, BANDS, stride=ROWS_M), :].astype(BF)
            total = total + dot(tables[c], rows)
        return total

    for r in range(EACH):
        piece[r * N : (r + 1) * N, :] = contracted(ROWS_T, SRC, r).astype(BF)
    last[:N, :] = contracted(ROWS_T, SRC, EACH)
    last[N:, :] = jnp.zeros((16, LANES), F32)
    band = lax.axis_index("band")
    piece[EACH * N :, :] = last[pl.ds((band & 7) * REST, 16), :].astype(BF)
    for t in range(QUART):
        quarter[t] = contracted(0, QUART, t).astype(BF)


def turned(scr, index):
    return jnp.concatenate(
        [
            scr[pl.ds(index, N, stride=PITCH), :].astype(BF),
            scr[pl.ds(index + 1, N, stride=PITCH), :].astype(BF),
        ],
        axis=1,
    )


def put(scr, index, values):
    scr[index * PITCH : index * PITCH + N, :] = values[:, :LANES]
    scr[(index + 1) * PITCH : (index + 1) * PITCH + N, :] = values[:, LANES:]


def side(ref, index):
    return jnp.concatenate([ref[index], ref[index + 1]], axis=1)


CHUNK = 5


def to_real(tile, out, table, expand, scr):
    for p in range(4):
        for lead in range(0, 10, CHUNK):
            rows = []
            for i in range(lead, lead + CHUNK):
                a = i * 5 + (160 * p) // LANES
                rows.append(jnp.concatenate([tile(a), tile(a + 1)], axis=1))
            res = dot(jnp.concatenate(rows, axis=0), expand[p])
            for j in range(CHUNK):
                put(scr, (lead + j) * 8 + 2 * p, res[j * N : (j + 1) * N])
    h = table[...]
    for x in range(0, N, 2):
        res = dot(h, turned(scr, x)).astype(BF)
        out[x] = res[:, :LANES]
        out[x + 1] = res[:, LANES:]


def target_kernel(own, got1, got2, got3, table, expand, out, scr, quarters):
    g = lax.axis_index("grp")
    for k, ref in enumerate((own, got1, got2, got3)):
        start = ((g - k) & 3) * QUART
        for t in range(QUART):
            quarters[start + t] = ref[t]
    to_real(lambda t: quarters[t], out, table, expand, scr)


PLACES = [(back, swap) for back in (0, 2, 4, 6) for swap in (False, True)]


def gather_tiles(same, other, pieces, lead, rest):
    band = lax.axis_index("band")
    core, z_at = band & 1, (band >> 1) & 7
    for refs, flip in ((same, 0), (other, 1)):
        couples = [ref.at[i] for ref in refs for i in range(ref.shape[0])]
        for j, (back, swap) in enumerate(PLACES):
            z = (z_at - back) & 7
            z = (z ^ 1) if swap else z
            origin = z * 2 + (core ^ flip)
            whole = couples[j // 2][j % 2]
            for r in range(EACH):
                pieces[lead + origin * EACH + r] = whole[r * N : (r + 1) * N]
            rest[pl.ds(origin * REST, REST), :] = whole[EACH * N :].astype(F32)[:REST]
    for j in range(TILES - WHOLE):
        pieces[lead + WHOLE + j] = rest[j * N : (j + 1) * N, :].astype(BF)


def one_source(pieces, k, target, source, before, partial, table, expand, twin, screen, scr_a, scr_b):
    to_real(lambda t: pieces[k * TILES + t], source, table, expand, scr_a)
    h = table[...]
    turn = twin[...]
    for lead in range(0, N, 2 * CHUNK):
        rows = []
        for x in range(lead, lead + 2 * CHUNK, 2):
            rows.append(dot(h, side(target, x) * side(source, x)).astype(BF))
        res = dot(jnp.concatenate(rows, axis=0), turn)
        for j in range(CHUNK):
            put(scr_a, lead + 2 * j, res[j * N : (j + 1) * N])
    for y in range(0, N, 2):
        spec = dot(h, turned(scr_a, y))
        weight = jnp.concatenate([screen[min(y, N - y)], screen[min(y + 1, N - 1 - y)]], axis=1)
        put(scr_b, y, dot(h, (spec * weight).astype(BF)))
    for lead in range(0, N, 2 * CHUNK):
        rows = [turned(scr_b, x) for x in range(lead, lead + 2 * CHUNK, 2)]
        res = dot(jnp.concatenate(rows, axis=0), turn).astype(BF)
        for j in range(CHUNK):
            pot = dot(h, res[j * N : (j + 1) * N])
            for e in range(2):
                x = lead + 2 * j + e
                term = source[x].astype(F32) * pot[:, e * LANES : (e + 1) * LANES]
                partial[x] = term if before is None else before[x] + term


def last_transform(partial, table, c0, c1, c2, scr, final):
    h = table[...]
    for x in range(0, N, 2):
        put(scr, x, dot(h, side(partial, x).astype(BF)))
    blocks = [[turned(scr, y + 2 * p) for p in range(4)] for y in range(0, N, 8)]
    for i in range(0, 10, CHUNK):
        eights = [jnp.concatenate(blocks[i + j], axis=1) for j in range(CHUNK)]
        r0 = dot(jnp.concatenate([v[:, :512] for v in eights], axis=0), c0[...]).astype(BF)
        r1 = dot(jnp.concatenate([v[:, 384:896] for v in eights], axis=0), c1[...]).astype(BF)
        r2 = dot(jnp.concatenate([v[:, 768:] for v in eights], axis=0), c2[...]).astype(BF)
        for j in range(CHUNK):
            t = (i + j) * 5
            rows = slice(j * N, (j + 1) * N)
            final[t] = r0[rows, :LANES]
            final[t + 1] = r0[rows, LANES:]
            final[t + 2] = r1[rows, :LANES]
            final[t + 3] = r1[rows, LANES:]
            final[t + 4] = r2[rows]
    final[TILES] = jnp.zeros((N, LANES), BF)
    final[TILES + 1] = jnp.zeros((N, LANES), BF)


def pairs_kernel(kinds, first, last, *refs):
    refs = list(refs)
    take = lambda n: [refs.pop(0) for _ in range(n)]
    sources = [(take(n), take(n)) for n in kinds]
    target, table, expand, twin, screen = take(5)
    before = None if first else take(1)[0]
    tables = take(3) if last else []
    outs = take(4) if last else take(1)
    source, scr_a, scr_b, pieces, rest = take(5)
    partial, final = take(2) if last else (outs[0], None)
    for i, (same, other) in enumerate(sources):
        gather_tiles(same, other, pieces, i * TILES, rest)
    work = (table, expand, twin, screen, scr_a, scr_b)
    if len(kinds) == 1:
        one_source(pieces, 0, target, source, before, partial, *work)
    else:
        partial[...] = before[...]

        def body(k, _):
            one_source(pieces, k, target, source, partial, partial, *work)
            return 0

        lax.fori_loop(0, len(kinds), body, 0)
    if last:
        last_transform(partial, table, *tables, scr_a, final)
        g = lax.axis_index("grp")
        for k, out in enumerate(outs):
            start = ((g + k) & 3) * QUART
            for t in range(QUART):
                out[t] = final[start + t]


def call_pairs(sources, target, tables, before=None, ends=None):
    kinds = tuple(len(same) for same, _ in sources)
    last = ends is not None
    operands = [v for same, other in sources for v in list(same) + list(other)]
    operands += [target, *tables] + ([] if before is None else [before]) + list(ends or [])
    scratch = [
        pltpu.VMEM((N, N, LANES), BF),
        pltpu.VMEM((N * PITCH, LANES), F32),
        pltpu.VMEM((N * PITCH, LANES), F32),
        pltpu.VMEM((len(kinds) * TILES, N, LANES), BF),
        pltpu.VMEM((SLAB * REST, LANES), F32),
    ]
    if last:
        scratch += [pltpu.VMEM((N, N, LANES), F32), pltpu.VMEM((TILES + 2, N, LANES), BF)]
    return pl.pallas_call(
        functools.partial(pairs_kernel, kinds, before is None, last),
        out_shape=tuple(shape((QUART, N, LANES)) for _ in range(4)) if last else shape((N, N, LANES), F32),
        in_specs=[VM] * len(operands),
        out_specs=(VM,) * 4 if last else VM,
        scratch_shapes=scratch,
        compiler_params=LARGE,
        cost_estimate=pl.CostEstimate(
            flops=6_000_000_000 * len(kinds), bytes_accessed=8_000_000, transcendentals=0
        ),
    )(*operands)


def select_kernel(own, got1, got2, got3, sel_t, msg, scr):
    tables = [sel_t[c] for c in range(SLOTS)]
    for t in range(QUART):
        total = (
            own[t].astype(F32) + got1[t].astype(F32) + got2[t].astype(F32) + got3[t].astype(F32)
        ).astype(BF)
        for c in range(SLOTS):
            scr[(c * QUART + t) * BANDS : (c * QUART + t + 1) * BANDS, :] = dot(tables[c], total)

    def body(d, _):
        msg[d] = scr[pl.ds(d, ROWS_T, stride=BANDS), :].astype(BF)
        return 0

    lax.fori_loop(0, BANDS, body, 0, unroll=8)


def rows_out_kernel(got, low, high, scr):
    def load(b, _):
        scr[pl.ds(pl.multiple_of(b * ROWS_T, 8), ROWS_T), :] = got[b].astype(F32)
        return 0

    lax.fori_loop(0, BANDS, load, 0, unroll=8)
    for c in range(SLOTS):
        for t in range(QUART):
            rows = scr[pl.ds(c * QUART + t, BANDS, stride=ROWS_T), :].astype(BF)
            low[c, :, t * LANES : (t + 1) * LANES] = rows[:HALF]
            high[c, :, t * LANES : (t + 1) * LANES] = rows[HALF:]


def join_kernel(*refs):
    out = refs[8]
    g = lax.axis_index("grp")
    wide = QUART * LANES
    short = (TILES - 3 * QUART) * LANES
    for k in range(4):
        origin = (g - k) & 3
        start = pl.multiple_of(origin * wide, LANES)

        @pl.when(origin < 3)
        def _():
            for c in range(SLOTS):
                for e in range(2):
                    out[c, e * HALF : (e + 1) * HALF, pl.ds(start, wide)] = refs[2 * k + e][c]

        @pl.when(origin == 3)
        def _():
            for c in range(SLOTS):
                for e in range(2):
                    out[c, e * HALF : (e + 1) * HALF, 3 * wide :] = refs[2 * k + e][c, :, :short]


VM = pl.BlockSpec(memory_space=pltpu.VMEM)
SM = pl.BlockSpec(memory_space=pltpu.SMEM)
ANY = pl.BlockSpec(memory_space=pl.ANY)
PARAMS = pltpu.CompilerParams(vmem_limit_bytes=16 * 1024 * 1024)
LARGE = pltpu.CompilerParams(vmem_limit_bytes=30 * 1024 * 1024)


def shape(dims, kind=BF):
    return jax.ShapeDtypeStruct(dims, kind)


def shift_grp(value, k):
    return lax.ppermute(value, "grp", [(i, (i + k) % GROUPS) for i in range(GROUPS)])


def swap_band(value, axis):
    bit = {"core": 1, "z": 2}[axis]
    return lax.ppermute(value, "band", [(i, i ^ bit) for i in range(BANDS)])


def shift_band(value, dx, dz, dc):
    moves = []
    for x in range(4):
        for z in range(8):
            for c in range(2):
                there = (((x + dx) % 4) * 8 + (z + dz) % 8) * 2 + (c + dc) % 2
                moves.append(((x * 8 + z) * 2 + c, there))
    return lax.ppermute(value, "band", moves)


def ring_gather(first, second, step):
    ahead = step(first, 1), step(second, 1)
    behind = step(first, 3), step(second, 3)
    far = step(ahead[0], 1), step(behind[1], 3)
    return [(first, second), ahead, far, behind]


def shards(stick_data, row_lengths, row_order, source_order):
    table = jnp.asarray(hartley_table())
    expand = jnp.asarray(expand_tables(hartley_table()))
    twin = jnp.asarray(pair_table(hartley_table()))
    c0, c1, c2 = (jnp.asarray(v) for v in compress_tables(hartley_table()))
    screen = jnp.asarray(screen_table())

    msg, sel, sel_t = pl.pallas_call(
        pack_kernel,
        out_shape=(
            shape((BANDS, ROWS_M, LANES)),
            shape((SLOTS, N, BANDS)),
            shape((SLOTS, BANDS, N)),
        ),
        in_specs=[SM, VM, VM, VM, VM],
        out_specs=(VM, VM, VM),
        scratch_shapes=[
            pltpu.VMEM((ROWS_T * BANDS, LANES), F32),
            pltpu.VMEM((BANDS * ROWS_S, LANES), F32),
        ],
        compiler_params=PARAMS,
    )(source_order, stick_data, row_lengths.reshape(1, BANDS), row_order.reshape(1, N), table)
    got = lax.all_to_all(msg, "band", 0, 0, tiled=True)
    quarter, piece = pl.pallas_call(
        rows_kernel,
        out_shape=(shape((QUART, N, LANES)), shape((PIECE, LANES))),
        in_specs=[VM, VM],
        out_specs=(VM, VM),
        scratch_shapes=[
            pltpu.VMEM((ROWS_M * BANDS, LANES), F32),
            pltpu.VMEM((N + 16, LANES), F32),
        ],
        compiler_params=PARAMS,
    )(got, sel)

    swapped = swap_band(piece, "z")
    quarters = [quarter] + [shift_grp(quarter, k) for k in range(1, 4)]
    couple = jnp.stack([piece, swapped])
    along_z = jnp.stack([couple] + [shift_band(couple, 0, k, 0) for k in (2, 4, 6)])

    along_z, *quarters = lax.optimization_barrier((along_z, *quarters))
    target = pl.pallas_call(
        target_kernel,
        out_shape=shape((N, N, LANES)),
        in_specs=[VM] * 6,
        out_specs=VM,
        scratch_shapes=[
            pltpu.VMEM((N * PITCH, LANES), F32),
            pltpu.VMEM((4 * QUART, N, LANES), BF),
        ],
        compiler_params=PARAMS,
    )(*quarters, table, expand)

    ahead, behind = shift_band(along_z, 1, 0, 0), shift_band(along_z, 3, 0, 0)
    flip = lambda v: shift_band(v, 0, 0, 1)

    tables = (table, expand, twin, screen)
    partial = call_pairs([([along_z], [flip(along_z)])], target, tables)
    ahead, behind, partial = lax.optimization_barrier((ahead, behind, partial))
    far = shift_band(ahead[:2], 1, 0, 0), shift_band(behind[2:], 3, 0, 0)
    ahead_flip, behind_flip = flip(ahead), flip(behind)
    partial = call_pairs([([ahead], [ahead_flip])], target, tables, before=partial)
    far_a, far_b, partial = lax.optimization_barrier((*far, partial))
    far, far_flip = (far_a, far_b), [flip(far_a), flip(far_b)]
    partial = call_pairs([([behind], [behind_flip])], target, tables, before=partial)
    outs = call_pairs([(far, far_flip)], target, tables, before=partial, ends=(c0, c1, c2))

    parts = [outs[0]] + [shift_grp(outs[k], k) for k in range(1, 4)]
    message = pl.pallas_call(
        select_kernel,
        out_shape=shape((BANDS, ROWS_T, LANES)),
        in_specs=[VM] * 5,
        out_specs=VM,
        scratch_shapes=[pltpu.VMEM((ROWS_T * BANDS, LANES), F32)],
        compiler_params=PARAMS,
    )(*parts, sel_t)

    received = lax.all_to_all(message, "band", 0, 0, tiled=True)
    low, high = pl.pallas_call(
        rows_out_kernel,
        out_shape=(shape((SLOTS, HALF, QUART * LANES)),) * 2,
        in_specs=[VM],
        out_specs=(VM, VM),
        scratch_shapes=[pltpu.VMEM((ROWS_T * BANDS, LANES), F32)],
        compiler_params=PARAMS,
    )(received)

    spread = ring_gather(low, high, shift_grp)
    return pl.pallas_call(
        join_kernel,
        out_shape=shape((SLOTS, BANDS, TILES * LANES)),
        in_specs=[VM] * 8,
        out_specs=VM,
        compiler_params=PARAMS,
    )(*[v for both in spread for v in both])


def solution(mesh):
    return jax.shard_map(
        shards,
        mesh=mesh,
        in_specs=(P("band", None, None), P(), P(), P()),
        out_specs=P("band", None, None),
        check_vma=False,
    )
```

```python
import functools
import math

import jax
import jax.numpy as jnp
import numpy as np
from jax import lax
from jax.experimental import pallas as pl
from jax.experimental.pallas import tpu as pltpu
from jax.sharding import PartitionSpec as P

N = 80
LANES = 128
TILES = 50
QUART = 13
SRC = 4
SLOTS = 3
BANDS = 64
GROUPS = 4
ROWS_T = 40
ROWS_S = 16
EACH = 3
SLAB = 16
WHOLE = EACH * SLAB
REST = 10
PIECE = 256
ROWS_M = ROWS_T + ROWS_S
HALF = BANDS // 2
PITCH = 88
BF = jnp.bfloat16
F32 = jnp.float32

coulomb_peak = 4.0
screen_square = 64.0


def hartley_table():
    index = np.arange(N)
    angles = (index[:, None] * index[None, :] % N).astype(np.float32) * np.float32(2.0 * math.pi / N)
    return ((np.cos(angles) + np.sin(angles)) / np.float32(math.sqrt(N))).astype(BF)


def expand_tables(table):
    out = np.zeros((4, 256, 256), BF)
    for p in range(4):
        off = 160 * p % LANES
        out[p, off : off + N, :N] = table
        out[p, off + N : off + 2 * N, LANES : LANES + N] = table
    return out


def pair_table(table):
    out = np.zeros((256, 256), BF)
    out[:N, :N] = table
    out[LANES : LANES + N, LANES : LANES + N] = table
    return out


def compress_tables(table):
    whole = np.zeros((1024, 640), BF)
    for y in range(8):
        whole[y * LANES : y * LANES + N, y * N : (y + 1) * N] = table
    return whole[:512, :256].copy(), whole[384:896, 256:512].copy(), whole[768:, 512:].copy()


def screen_table():
    freq = np.minimum(np.arange(N), N - np.arange(N)).astype(np.float32)
    sq = freq * freq
    total = sq[:41, None, None] + sq[None, :, None] + sq[None, None, :]
    out = np.zeros((41, N, LANES), np.float32)
    out[:, :, :N] = np.float32(coulomb_peak) / (np.float32(1.0) + total / np.float32(screen_square))
    return out


def dot(a, b):
    return jnp.dot(a, b, preferred_element_type=F32)


def dot_tn(a, b):
    return lax.dot_general(a, b, (((0,), (0,)), ((), ())), preferred_element_type=F32)


def pack_kernel(
    order_h, stick_h, lengths_h, rows_h, table_h, msg, sel, sel_t,
    order_s, stick, lengths, order_v, table, scr, scr_s, sem,
):
    pairs = (
        (order_h, order_s), (lengths_h, lengths), (rows_h, order_v), (table_h, table), (stick_h, stick)
    )
    copies = [pltpu.make_async_copy(a, b, sem.at[i]) for i, (a, b) in enumerate(pairs)]
    for copy in copies:
        copy.start()
    for copy in copies[:4]:
        copy.wait()
    g = lax.axis_index("grp")
    lens = lengths[...]
    d0 = lax.broadcasted_iota(jnp.int32, (BANDS, BANDS), 0)
    d1 = lax.broadcasted_iota(jnp.int32, (BANDS, BANDS), 1)
    before = jnp.where(d0 < d1, 1.0, 0.0).astype(BF)
    lens8 = jnp.broadcast_to(lens, (8, BANDS)).astype(F32)
    starts = dot(lens8.astype(BF), before)[:1]
    q0 = lax.broadcasted_iota(jnp.int32, (N, N), 0)
    perm = jnp.where(jnp.broadcast_to(order_v[...], (N, N)) == q0, 1.0, 0.0).astype(BF)
    permuted = dot(table[...], perm).astype(BF)
    place = lax.broadcasted_iota(jnp.int32, (N, BANDS), 0).astype(F32)
    for c in range(SLOTS):
        hit = (place == jnp.broadcast_to(starts + c, (N, BANDS))) & (
            jnp.broadcast_to(lens8[:1], (N, BANDS)) > c
        )
        one = jnp.where(hit, 1.0, 0.0).astype(BF)
        sel[c] = dot(permuted, one).astype(BF)
        sel_t[c] = lax.dot_general(
            one, permuted, (((0,), (1,)), ((), ())), preferred_element_type=F32
        ).astype(BF)
    copies[4].wait()
    first = QUART * g
    for c in range(SLOTS):

        def body(t, _):
            lane = pl.multiple_of(jnp.minimum(first + t, TILES - 1) * LANES, LANES)
            row = pl.multiple_of((c * QUART + t) * BANDS, BANDS)
            scr[pl.ds(row, BANDS), :] = stick[c, :, pl.ds(lane, LANES)].astype(F32)
            return 0

        lax.fori_loop(0, QUART, body, 0, unroll=True)

    b1 = lax.broadcasted_iota(jnp.int32, (16, BANDS), 1)
    r1 = lax.broadcasted_iota(jnp.int32, (16, BANDS), 0)
    pick = jnp.zeros((16, BANDS), F32)
    for k in range(SRC):
        pick = jnp.where((r1 == k) & (b1 == order_s[g * SRC + k]), 1.0, pick)
    pick = pick.astype(BF)
    for c in range(SLOTS):
        for u in range(TILES // 2):
            got = dot(pick, stick[c, :, u * 256 : u * 256 + 256])
            for h in range(2):
                for k in range(SRC):
                    t = 2 * u + h
                    line = got[k : k + 1, h * LANES : (h + 1) * LANES]
                    if t < WHOLE:
                        places = [(t // EACH, t % EACH)]
                    else:
                        places = [(8 * (t - WHOLE) + i, EACH) for i in range(8)]
                    for d, r in places:
                        row = (k * SLAB + d) * ROWS_S + c * SRC + r
                        scr_s[row : row + 1, :] = line

    def out_body(b, _):
        mine = scr[pl.ds(b, ROWS_T, stride=BANDS), :]
        tile = scr_s[pl.ds(pl.multiple_of(b * ROWS_S, 8), ROWS_S), :]
        msg[b] = jnp.concatenate([mine, tile], axis=0).astype(BF)
        return 0

    lax.fori_loop(0, BANDS, out_body, 0, unroll=8)


def rows_kernel(got, sel, quarter, piece, scr, last):
    def load(d, _):
        scr[pl.ds(pl.multiple_of(d * ROWS_M, 8), ROWS_M), :] = got[d].astype(F32)
        return 0

    lax.fori_loop(0, BANDS, load, 0, unroll=8)
    tables = [sel[c] for c in range(SLOTS)]

    def contracted(first, count, t):
        total = jnp.zeros((N, LANES), F32)
        for c in range(SLOTS):
            rows = scr[pl.ds(first + c * count + t, BANDS, stride=ROWS_M), :].astype(BF)
            total = total + dot(tables[c], rows)
        return total

    for r in range(EACH):
        piece[r * N : (r + 1) * N, :] = contracted(ROWS_T, SRC, r).astype(BF)
    last[:N, :] = contracted(ROWS_T, SRC, EACH)
    last[N:, :] = jnp.zeros((16, LANES), F32)
    band = lax.axis_index("band")
    piece[EACH * N :, :] = last[pl.ds((band & 7) * REST, 16), :].astype(BF)
    for t in range(QUART):
        quarter[t] = contracted(0, QUART, t).astype(BF)


def turned(scr, index):
    return jnp.concatenate(
        [
            scr[pl.ds(index, N, stride=PITCH), :].astype(BF),
            scr[pl.ds(index + 1, N, stride=PITCH), :].astype(BF),
        ],
        axis=1,
    )


def put(scr, index, values):
    scr[index * PITCH : index * PITCH + N, :] = values[:, :LANES]
    scr[(index + 1) * PITCH : (index + 1) * PITCH + N, :] = values[:, LANES:]


def side(ref, index):
    return jnp.concatenate([ref[index], ref[index + 1]], axis=1)


CHUNK = 5


def to_real(tile, out, table, expand, scr):
    for p in range(4):
        for lead in range(0, 10, CHUNK):
            rows = []
            for i in range(lead, lead + CHUNK):
                a = i * 5 + (160 * p) // LANES
                rows.append(jnp.concatenate([tile(a), tile(a + 1)], axis=1))
            res = dot(jnp.concatenate(rows, axis=0), expand[p])
            for j in range(CHUNK):
                put(scr, (lead + j) * 8 + 2 * p, res[j * N : (j + 1) * N])
    h = table[...]
    for x in range(0, N, 2):
        res = dot(h, turned(scr, x)).astype(BF)
        out[x] = res[:, :LANES]
        out[x + 1] = res[:, LANES:]


def target_kernel(own, got1, got2, got3, table, expand, out, scr, quarters):
    g = lax.axis_index("grp")
    for k, ref in enumerate((own, got1, got2, got3)):
        start = ((g - k) & 3) * QUART
        for t in range(QUART):
            quarters[start + t] = ref[t]
    to_real(lambda t: quarters[t], out, table, expand, scr)


PLACES = [(back, swap) for back in (0, 2, 4, 6) for swap in (False, True)]


def gather_tiles(same, other, pieces, lead, rest):
    band = lax.axis_index("band")
    core, z_at = band & 1, (band >> 1) & 7
    for refs, flip in ((same, 0), (other, 1)):
        couples = [ref.at[i] for ref in refs for i in range(ref.shape[0])]
        for j, (back, swap) in enumerate(PLACES):
            z = (z_at - back) & 7
            z = (z ^ 1) if swap else z
            origin = z * 2 + (core ^ flip)
            whole = couples[j // 2][j % 2]
            for r in range(EACH):
                pieces[lead + origin * EACH + r] = whole[r * N : (r + 1) * N]
            rest[pl.ds(origin * REST, REST), :] = whole[EACH * N :].astype(F32)[:REST]
    for j in range(TILES - WHOLE):
        pieces[lead + WHOLE + j] = rest[j * N : (j + 1) * N, :].astype(BF)


def one_source(pieces, k, target, source, before, partial, table, expand, twin, screen, scr_a, scr_b):
    to_real(lambda t: pieces[k * TILES + t], source, table, expand, scr_a)
    h = table[...]
    turn = twin[...]
    for lead in range(0, N, 2 * CHUNK):
        rows = []
        for x in range(lead, lead + 2 * CHUNK, 2):
            rows.append(dot(h, side(target, x) * side(source, x)).astype(BF))
        res = dot(jnp.concatenate(rows, axis=0), turn)
        for j in range(CHUNK):
            put(scr_a, lead + 2 * j, res[j * N : (j + 1) * N])
    for y in range(0, N, 2):
        spec = dot(h, turned(scr_a, y))
        weight = jnp.concatenate([screen[min(y, N - y)], screen[min(y + 1, N - 1 - y)]], axis=1)
        put(scr_b, y, dot(h, (spec * weight).astype(BF)))
    for lead in range(0, N, 2 * CHUNK):
        rows = [turned(scr_b, x) for x in range(lead, lead + 2 * CHUNK, 2)]
        res = dot(jnp.concatenate(rows, axis=0), turn).astype(BF)
        for j in range(CHUNK):
            pot = dot(h, res[j * N : (j + 1) * N])
            for e in range(2):
                x = lead + 2 * j + e
                term = source[x].astype(F32) * pot[:, e * LANES : (e + 1) * LANES]
                partial[x] = term if before is None else before[x] + term


def last_transform(partial, table, c0, c1, c2, scr, final):
    h = table[...]
    for x in range(0, N, 2):
        put(scr, x, dot(h, side(partial, x).astype(BF)))
    blocks = [[turned(scr, y + 2 * p) for p in range(4)] for y in range(0, N, 8)]
    for i in range(0, 10, CHUNK):
        eights = [jnp.concatenate(blocks[i + j], axis=1) for j in range(CHUNK)]
        r0 = dot(jnp.concatenate([v[:, :512] for v in eights], axis=0), c0[...]).astype(BF)
        r1 = dot(jnp.concatenate([v[:, 384:896] for v in eights], axis=0), c1[...]).astype(BF)
        r2 = dot(jnp.concatenate([v[:, 768:] for v in eights], axis=0), c2[...]).astype(BF)
        for j in range(CHUNK):
            t = (i + j) * 5
            rows = slice(j * N, (j + 1) * N)
            final[t] = r0[rows, :LANES]
            final[t + 1] = r0[rows, LANES:]
            final[t + 2] = r1[rows, :LANES]
            final[t + 3] = r1[rows, LANES:]
            final[t + 4] = r2[rows]
    final[TILES] = jnp.zeros((N, LANES), BF)
    final[TILES + 1] = jnp.zeros((N, LANES), BF)


def pairs_kernel(kinds, first, last, *refs):
    refs = list(refs)
    take = lambda n: [refs.pop(0) for _ in range(n)]
    sources = [(take(n), take(n)) for n in kinds]
    target, table, expand, twin, screen = take(5)
    before = None if first else take(1)[0]
    tables = take(3) if last else []
    outs = take(4) if last else take(1)
    source, scr_a, scr_b, pieces, rest = take(5)
    partial, final = take(2) if last else (outs[0], None)
    for i, (same, other) in enumerate(sources):
        gather_tiles(same, other, pieces, i * TILES, rest)
    work = (table, expand, twin, screen, scr_a, scr_b)
    if len(kinds) == 1:
        one_source(pieces, 0, target, source, before, partial, *work)
    else:
        partial[...] = before[...]

        def body(k, _):
            one_source(pieces, k, target, source, partial, partial, *work)
            return 0

        lax.fori_loop(0, len(kinds), body, 0)
    if last:
        last_transform(partial, table, *tables, scr_a, final)
        g = lax.axis_index("grp")
        for k, out in enumerate(outs):
            start = ((g + k) & 3) * QUART
            for t in range(QUART):
                out[t] = final[start + t]


def call_pairs(sources, target, tables, before=None, ends=None):
    kinds = tuple(len(same) for same, _ in sources)
    last = ends is not None
    operands = [v for same, other in sources for v in list(same) + list(other)]
    operands += [target, *tables] + ([] if before is None else [before]) + list(ends or [])
    scratch = [
        pltpu.VMEM((N, N, LANES), BF),
        pltpu.VMEM((N * PITCH, LANES), F32),
        pltpu.VMEM((N * PITCH, LANES), F32),
        pltpu.VMEM((len(kinds) * TILES, N, LANES), BF),
        pltpu.VMEM((SLAB * REST, LANES), F32),
    ]
    if last:
        scratch += [pltpu.VMEM((N, N, LANES), F32), pltpu.VMEM((TILES + 2, N, LANES), BF)]
    return pl.pallas_call(
        functools.partial(pairs_kernel, kinds, before is None, last),
        out_shape=tuple(shape((QUART, N, LANES)) for _ in range(4)) if last else shape((N, N, LANES), F32),
        in_specs=[VM] * len(operands),
        out_specs=(VM,) * 4 if last else VM,
        scratch_shapes=scratch,
        compiler_params=LARGE,
        cost_estimate=pl.CostEstimate(
            flops=6_000_000_000 * len(kinds), bytes_accessed=8_000_000, transcendentals=0
        ),
    )(*operands)


def select_kernel(own, got1, got2, got3, sel_t, msg, scr):
    tables = [sel_t[c] for c in range(SLOTS)]
    for t in range(QUART):
        total = (
            own[t].astype(F32) + got1[t].astype(F32) + got2[t].astype(F32) + got3[t].astype(F32)
        ).astype(BF)
        for c in range(SLOTS):
            scr[(c * QUART + t) * BANDS : (c * QUART + t + 1) * BANDS, :] = dot(tables[c], total)

    def body(d, _):
        msg[d] = scr[pl.ds(d, ROWS_T, stride=BANDS), :].astype(BF)
        return 0

    lax.fori_loop(0, BANDS, body, 0, unroll=8)


def rows_out_kernel(got, low, high, scr):
    def load(b, _):
        scr[pl.ds(pl.multiple_of(b * ROWS_T, 8), ROWS_T), :] = got[b].astype(F32)
        return 0

    lax.fori_loop(0, BANDS, load, 0, unroll=8)
    for c in range(SLOTS):
        for t in range(QUART):
            rows = scr[pl.ds(c * QUART + t, BANDS, stride=ROWS_T), :].astype(BF)
            low[c, :, t * LANES : (t + 1) * LANES] = rows[:HALF]
            high[c, :, t * LANES : (t + 1) * LANES] = rows[HALF:]


def join_kernel(*refs):
    out = refs[8]
    g = lax.axis_index("grp")
    wide = QUART * LANES
    short = (TILES - 3 * QUART) * LANES
    for k in range(4):
        origin = (g - k) & 3
        start = pl.multiple_of(origin * wide, LANES)

        @pl.when(origin < 3)
        def _():
            for c in range(SLOTS):
                for e in range(2):
                    out[c, e * HALF : (e + 1) * HALF, pl.ds(start, wide)] = refs[2 * k + e][c]

        @pl.when(origin == 3)
        def _():
            for c in range(SLOTS):
                for e in range(2):
                    out[c, e * HALF : (e + 1) * HALF, 3 * wide :] = refs[2 * k + e][c, :, :short]


VM = pl.BlockSpec(memory_space=pltpu.VMEM)
HB = pl.BlockSpec(memory_space=pltpu.HBM)
PARAMS = pltpu.CompilerParams(vmem_limit_bytes=16 * 1024 * 1024)
WHOLE_VMEM = pltpu.CompilerParams(vmem_limit_bytes=60 * 1024 * 1024)
LARGE = pltpu.CompilerParams(vmem_limit_bytes=30 * 1024 * 1024)


def shape(dims, kind=BF):
    return jax.ShapeDtypeStruct(dims, kind)


def shift_grp(value, k):
    return lax.ppermute(value, "grp", [(i, (i + k) % GROUPS) for i in range(GROUPS)])


def swap_band(value, axis):
    bit = {"core": 1, "z": 2}[axis]
    return lax.ppermute(value, "band", [(i, i ^ bit) for i in range(BANDS)])


def shift_band(value, dx, dz, dc):
    moves = []
    for x in range(4):
        for z in range(8):
            for c in range(2):
                there = (((x + dx) % 4) * 8 + (z + dz) % 8) * 2 + (c + dc) % 2
                moves.append(((x * 8 + z) * 2 + c, there))
    return lax.ppermute(value, "band", moves)


def ring_gather(first, second, step):
    ahead = step(first, 1), step(second, 1)
    behind = step(first, 3), step(second, 3)
    far = step(ahead[0], 1), step(behind[1], 3)
    return [(first, second), ahead, far, behind]


def shards(stick_data, row_lengths, row_order, source_order):
    table = jnp.asarray(hartley_table())
    expand = jnp.asarray(expand_tables(hartley_table()))
    twin = jnp.asarray(pair_table(hartley_table()))
    c0, c1, c2 = (jnp.asarray(v) for v in compress_tables(hartley_table()))
    screen = jnp.asarray(screen_table())

    msg, sel, sel_t = pl.pallas_call(
        pack_kernel,
        out_shape=(
            shape((BANDS, ROWS_M, LANES)),
            shape((SLOTS, N, BANDS)),
            shape((SLOTS, BANDS, N)),
        ),
        in_specs=[HB] * 5,
        out_specs=(VM, VM, VM),
        scratch_shapes=[
            pltpu.SMEM((BANDS,), jnp.int32),
            pltpu.VMEM((SLOTS, BANDS, TILES * LANES), BF),
            pltpu.VMEM((1, BANDS), jnp.int32),
            pltpu.VMEM((1, N), jnp.int32),
            pltpu.VMEM((N, N), BF),
            pltpu.VMEM((ROWS_T * BANDS, LANES), F32),
            pltpu.VMEM((BANDS * ROWS_S, LANES), F32),
            pltpu.SemaphoreType.DMA((5,)),
        ],
        compiler_params=WHOLE_VMEM,
    )(source_order, stick_data, row_lengths.reshape(1, BANDS), row_order.reshape(1, N), table)
    got = lax.all_to_all(msg, "band", 0, 0, tiled=True)
    quarter, piece = pl.pallas_call(
        rows_kernel,
        out_shape=(shape((QUART, N, LANES)), shape((PIECE, LANES))),
        in_specs=[VM, VM],
        out_specs=(VM, VM),
        scratch_shapes=[
            pltpu.VMEM((ROWS_M * BANDS, LANES), F32),
            pltpu.VMEM((N + 16, LANES), F32),
        ],
        compiler_params=PARAMS,
    )(got, sel)

    swapped = swap_band(piece, "z")
    couple = jnp.stack([piece, swapped])
    nearest = shift_band(couple, 0, 2, 0)
    others = [shift_band(couple, 0, k, 0) for k in (4, 6)]
    nearest, again = lax.optimization_barrier((nearest, quarter))
    behind_one, opposite, before_one = shift_grp(quarter, 1), shift_grp(quarter, 2), shift_grp(again, 3)
    along_z = jnp.stack([couple, nearest, *others])
    along_z, behind_one, opposite = lax.optimization_barrier((along_z, behind_one, opposite))
    quarters = [quarter, behind_one, opposite, before_one]

    target = pl.pallas_call(
        target_kernel,
        out_shape=shape((N, N, LANES)),
        in_specs=[VM] * 6,
        out_specs=VM,
        scratch_shapes=[
            pltpu.VMEM((N * PITCH, LANES), F32),
            pltpu.VMEM((4 * QUART, N, LANES), BF),
        ],
        compiler_params=PARAMS,
    )(*quarters, table, expand)

    ahead, behind = shift_band(along_z, 1, 0, 0), shift_band(along_z, 3, 0, 0)
    flip = lambda v: shift_band(v, 0, 0, 1)

    tables = (table, expand, twin, screen)
    partial = call_pairs([([along_z], [flip(along_z)])], target, tables)
    ahead, behind, partial = lax.optimization_barrier((ahead, behind, partial))
    far = shift_band(ahead[:2], 1, 0, 0), shift_band(behind[2:], 3, 0, 0)
    ahead_flip, behind_flip = flip(ahead), flip(behind)
    partial = call_pairs([([ahead], [ahead_flip])], target, tables, before=partial)
    far_a, far_b, partial = lax.optimization_barrier((*far, partial))
    far, far_flip = (far_a, far_b), [flip(far_a), flip(far_b)]
    partial = call_pairs([([behind], [behind_flip])], target, tables, before=partial)
    outs = call_pairs([(far, far_flip)], target, tables, before=partial, ends=(c0, c1, c2))

    parts = [outs[0]] + [shift_grp(outs[k], k) for k in (2, 1, 3)]
    message = pl.pallas_call(
        select_kernel,
        out_shape=shape((BANDS, ROWS_T, LANES)),
        in_specs=[VM] * 5,
        out_specs=VM,
        scratch_shapes=[pltpu.VMEM((ROWS_T * BANDS, LANES), F32)],
        compiler_params=PARAMS,
    )(*parts, sel_t)

    received = lax.all_to_all(message, "band", 0, 0, tiled=True)
    low, high = pl.pallas_call(
        rows_out_kernel,
        out_shape=(shape((SLOTS, HALF, QUART * LANES)),) * 2,
        in_specs=[VM],
        out_specs=(VM, VM),
        scratch_shapes=[pltpu.VMEM((ROWS_T * BANDS, LANES), F32)],
        compiler_params=PARAMS,
    )(received)

    spread = ring_gather(low, high, shift_grp)
    return pl.pallas_call(
        join_kernel,
        out_shape=shape((SLOTS, BANDS, TILES * LANES)),
        in_specs=[VM] * 8,
        out_specs=VM,
        compiler_params=PARAMS,
    )(*[v for both in spread for v in both])


def solution(mesh):
    return jax.shard_map(
        shards,
        mesh=mesh,
        in_specs=(P("band", None, None), P(), P(), P()),
        out_specs=P("band", None, None),
        check_vma=False,
    )
```

```python
import functools
import math

import jax
import jax.numpy as jnp
import numpy as np
from jax import lax
from jax.experimental import pallas as pl
from jax.experimental.pallas import tpu as pltpu
from jax.sharding import PartitionSpec as P

N = 80
LANES = 128
TILES = 50
QUART = 13
SRC = 4
SLOTS = 3
BANDS = 64
GROUPS = 4
ROWS_T = 40
ROWS_S = 16
EACH = 3
SLAB = 16
WHOLE = EACH * SLAB
REST = 10
PIECE = 256
ROWS_M = ROWS_T + ROWS_S
HALF = BANDS // 2
PITCH = 88
BF = jnp.bfloat16
F32 = jnp.float32

coulomb_peak = 4.0
screen_square = 64.0


def hartley_table():
    index = np.arange(N)
    angles = (index[:, None] * index[None, :] % N).astype(np.float32) * np.float32(2.0 * math.pi / N)
    return ((np.cos(angles) + np.sin(angles)) / np.float32(math.sqrt(N))).astype(BF)


def expand_tables(table):
    out = np.zeros((4, 256, 256), BF)
    for p in range(4):
        off = 160 * p % LANES
        out[p, off : off + N, :N] = table
        out[p, off + N : off + 2 * N, LANES : LANES + N] = table
    return out


def pair_table(table):
    out = np.zeros((256, 256), BF)
    out[:N, :N] = table
    out[LANES : LANES + N, LANES : LANES + N] = table
    return out


def compress_tables(table):
    whole = np.zeros((1024, 640), BF)
    for y in range(8):
        whole[y * LANES : y * LANES + N, y * N : (y + 1) * N] = table
    return whole[:512, :256].copy(), whole[384:896, 256:512].copy(), whole[768:, 512:].copy()


def screen_table():
    freq = np.minimum(np.arange(N), N - np.arange(N)).astype(np.float32)
    sq = freq * freq
    total = sq[:41, None, None] + sq[None, :, None] + sq[None, None, :]
    out = np.zeros((41, N, LANES), np.float32)
    out[:, :, :N] = np.float32(coulomb_peak) / (np.float32(1.0) + total / np.float32(screen_square))
    return out


def dot(a, b):
    return jnp.dot(a, b, preferred_element_type=F32)


def dot_tn(a, b):
    return lax.dot_general(a, b, (((0,), (0,)), ((), ())), preferred_element_type=F32)


def pack_kernel(
    order_h, stick_h, msg, order_s, stick, scr, scr_s, sem,
):
    pairs = (order_h, order_s), (stick_h, stick)
    copies = [pltpu.make_async_copy(a, b, sem.at[i]) for i, (a, b) in enumerate(pairs)]
    for copy in copies:
        copy.start()
    for copy in copies:
        copy.wait()
    g = lax.axis_index("grp")
    first = QUART * g
    for c in range(SLOTS):

        def body(t, _):
            lane = pl.multiple_of(jnp.minimum(first + t, TILES - 1) * LANES, LANES)
            row = pl.multiple_of((c * QUART + t) * BANDS, BANDS)
            scr[pl.ds(row, BANDS), :] = stick[c, :, pl.ds(lane, LANES)].astype(F32)
            return 0

        lax.fori_loop(0, QUART, body, 0, unroll=True)

    b1 = lax.broadcasted_iota(jnp.int32, (16, BANDS), 1)
    r1 = lax.broadcasted_iota(jnp.int32, (16, BANDS), 0)
    pick = jnp.zeros((16, BANDS), F32)
    for k in range(SRC):
        pick = jnp.where((r1 == k) & (b1 == order_s[g * SRC + k]), 1.0, pick)
    pick = pick.astype(BF)
    for c in range(SLOTS):
        for u in range(TILES // 2):
            got = dot(pick, stick[c, :, u * 256 : u * 256 + 256])
            for h in range(2):
                for k in range(SRC):
                    t = 2 * u + h
                    line = got[k : k + 1, h * LANES : (h + 1) * LANES]
                    if t < WHOLE:
                        places = [(t // EACH, t % EACH)]
                    else:
                        places = [(8 * (t - WHOLE) + i, EACH) for i in range(8)]
                    for d, r in places:
                        row = (k * SLAB + d) * ROWS_S + c * SRC + r
                        scr_s[row : row + 1, :] = line

    def out_body(b, _):
        mine = scr[pl.ds(b, ROWS_T, stride=BANDS), :]
        tile = scr_s[pl.ds(pl.multiple_of(b * ROWS_S, 8), ROWS_S), :]
        msg[b] = jnp.concatenate([mine, tile], axis=0).astype(BF)
        return 0

    lax.fori_loop(0, BANDS, out_body, 0, unroll=8)


def rows_kernel(got, lengths, order_v, table, quarter, piece, sel_t, scr, last):
    lens = lengths[...]
    d0 = lax.broadcasted_iota(jnp.int32, (BANDS, BANDS), 0)
    d1 = lax.broadcasted_iota(jnp.int32, (BANDS, BANDS), 1)
    before = jnp.where(d0 < d1, 1.0, 0.0).astype(BF)
    lens8 = jnp.broadcast_to(lens, (8, BANDS)).astype(F32)
    starts = dot(lens8.astype(BF), before)[:1]
    q0 = lax.broadcasted_iota(jnp.int32, (N, N), 0)
    perm = jnp.where(jnp.broadcast_to(order_v[...], (N, N)) == q0, 1.0, 0.0).astype(BF)
    permuted = dot(table[...], perm).astype(BF)
    place = lax.broadcasted_iota(jnp.int32, (N, BANDS), 0).astype(F32)
    tables = []
    for c in range(SLOTS):
        hit = (place == jnp.broadcast_to(starts + c, (N, BANDS))) & (
            jnp.broadcast_to(lens8[:1], (N, BANDS)) > c
        )
        one = jnp.where(hit, 1.0, 0.0).astype(BF)
        tables.append(dot(permuted, one).astype(BF))
        sel_t[c] = lax.dot_general(
            one, permuted, (((0,), (1,)), ((), ())), preferred_element_type=F32
        ).astype(BF)
    def load(d, _):
        scr[pl.ds(pl.multiple_of(d * ROWS_M, 8), ROWS_M), :] = got[d].astype(F32)
        return 0

    lax.fori_loop(0, BANDS, load, 0, unroll=8)

    def contracted(first, count, t):
        total = jnp.zeros((N, LANES), F32)
        for c in range(SLOTS):
            rows = scr[pl.ds(first + c * count + t, BANDS, stride=ROWS_M), :].astype(BF)
            total = total + dot(tables[c], rows)
        return total

    for r in range(EACH):
        piece[r * N : (r + 1) * N, :] = contracted(ROWS_T, SRC, r).astype(BF)
    last[:N, :] = contracted(ROWS_T, SRC, EACH)
    last[N:, :] = jnp.zeros((16, LANES), F32)
    band = lax.axis_index("band")
    piece[EACH * N :, :] = last[pl.ds((band & 7) * REST, 16), :].astype(BF)
    for t in range(QUART):
        quarter[t] = contracted(0, QUART, t).astype(BF)


def turned(scr, index):
    return jnp.concatenate(
        [
            scr[pl.ds(index, N, stride=PITCH), :].astype(BF),
            scr[pl.ds(index + 1, N, stride=PITCH), :].astype(BF),
        ],
        axis=1,
    )


def put(scr, index, values):
    scr[index * PITCH : index * PITCH + N, :] = values[:, :LANES]
    scr[(index + 1) * PITCH : (index + 1) * PITCH + N, :] = values[:, LANES:]


def side(ref, index):
    return jnp.concatenate([ref[index], ref[index + 1]], axis=1)


CHUNK = 5


def to_real(tile, out, table, expand, scr):
    for p in range(4):
        for lead in range(0, 10, CHUNK):
            rows = []
            for i in range(lead, lead + CHUNK):
                a = i * 5 + (160 * p) // LANES
                rows.append(jnp.concatenate([tile(a), tile(a + 1)], axis=1))
            res = dot(jnp.concatenate(rows, axis=0), expand[p])
            for j in range(CHUNK):
                put(scr, (lead + j) * 8 + 2 * p, res[j * N : (j + 1) * N])
    h = table[...]
    for x in range(0, N, 2):
        res = dot(h, turned(scr, x)).astype(BF)
        out[x] = res[:, :LANES]
        out[x + 1] = res[:, LANES:]


def target_kernel(own, got1, got2, got3, table, expand, out, scr, quarters):
    g = lax.axis_index("grp")
    for k, ref in enumerate((own, got1, got2, got3)):
        start = ((g - k) & 3) * QUART
        for t in range(QUART):
            quarters[start + t] = ref[t]
    to_real(lambda t: quarters[t], out, table, expand, scr)


PLACES = [(back, swap) for back in (0, 2, 4, 6) for swap in (False, True)]


def gather_tiles(same, other, pieces, lead, rest):
    band = lax.axis_index("band")
    core, z_at = band & 1, (band >> 1) & 7
    for refs, flip in ((same, 0), (other, 1)):
        couples = [ref.at[i] for ref in refs for i in range(ref.shape[0])]
        for j, (back, swap) in enumerate(PLACES):
            z = (z_at - back) & 7
            z = (z ^ 1) if swap else z
            origin = z * 2 + (core ^ flip)
            whole = couples[j // 2][j % 2]
            for r in range(EACH):
                pieces[lead + origin * EACH + r] = whole[r * N : (r + 1) * N]
            rest[pl.ds(origin * REST, REST), :] = whole[EACH * N :].astype(F32)[:REST]
    for j in range(TILES - WHOLE):
        pieces[lead + WHOLE + j] = rest[j * N : (j + 1) * N, :].astype(BF)


def one_source(pieces, k, target, source, before, partial, table, expand, twin, screen, scr_a, scr_b):
    to_real(lambda t: pieces[k * TILES + t], source, table, expand, scr_a)
    h = table[...]
    turn = twin[...]
    for lead in range(0, N, 2 * CHUNK):
        rows = []
        for x in range(lead, lead + 2 * CHUNK, 2):
            rows.append(dot(h, side(target, x) * side(source, x)).astype(BF))
        res = dot(jnp.concatenate(rows, axis=0), turn)
        for j in range(CHUNK):
            put(scr_a, lead + 2 * j, res[j * N : (j + 1) * N])
    for y in range(0, N, 2):
        spec = dot(h, turned(scr_a, y))
        weight = jnp.concatenate([screen[min(y, N - y)], screen[min(y + 1, N - 1 - y)]], axis=1)
        put(scr_b, y, dot(h, (spec * weight).astype(BF)))
    for lead in range(0, N, 2 * CHUNK):
        rows = [turned(scr_b, x) for x in range(lead, lead + 2 * CHUNK, 2)]
        res = dot(jnp.concatenate(rows, axis=0), turn).astype(BF)
        for j in range(CHUNK):
            pot = dot(h, res[j * N : (j + 1) * N])
            for e in range(2):
                x = lead + 2 * j + e
                term = source[x].astype(F32) * pot[:, e * LANES : (e + 1) * LANES]
                partial[x] = term if before is None else before[x] + term


def last_transform(partial, table, c0, c1, c2, scr, final):
    h = table[...]
    for x in range(0, N, 2):
        put(scr, x, dot(h, side(partial, x).astype(BF)))
    blocks = [[turned(scr, y + 2 * p) for p in range(4)] for y in range(0, N, 8)]
    for i in range(0, 10, CHUNK):
        eights = [jnp.concatenate(blocks[i + j], axis=1) for j in range(CHUNK)]
        r0 = dot(jnp.concatenate([v[:, :512] for v in eights], axis=0), c0[...]).astype(BF)
        r1 = dot(jnp.concatenate([v[:, 384:896] for v in eights], axis=0), c1[...]).astype(BF)
        r2 = dot(jnp.concatenate([v[:, 768:] for v in eights], axis=0), c2[...]).astype(BF)
        for j in range(CHUNK):
            t = (i + j) * 5
            rows = slice(j * N, (j + 1) * N)
            final[t] = r0[rows, :LANES]
            final[t + 1] = r0[rows, LANES:]
            final[t + 2] = r1[rows, :LANES]
            final[t + 3] = r1[rows, LANES:]
            final[t + 4] = r2[rows]
    final[TILES] = jnp.zeros((N, LANES), BF)
    final[TILES + 1] = jnp.zeros((N, LANES), BF)


def pairs_kernel(kinds, first, last, *refs):
    refs = list(refs)
    take = lambda n: [refs.pop(0) for _ in range(n)]
    sources = [(take(n), take(n)) for n in kinds]
    target, table, expand, twin, screen = take(5)
    before = None if first else take(1)[0]
    tables = take(3) if last else []
    outs = take(4) if last else take(1)
    source, scr_a, scr_b, pieces, rest = take(5)
    partial, final = take(2) if last else (outs[0], None)
    for i, (same, other) in enumerate(sources):
        gather_tiles(same, other, pieces, i * TILES, rest)
    work = (table, expand, twin, screen, scr_a, scr_b)
    if len(kinds) == 1:
        one_source(pieces, 0, target, source, before, partial, *work)
    else:
        partial[...] = before[...]

        def body(k, _):
            one_source(pieces, k, target, source, partial, partial, *work)
            return 0

        lax.fori_loop(0, len(kinds), body, 0)
    if last:
        last_transform(partial, table, *tables, scr_a, final)
        g = lax.axis_index("grp")
        for k, out in enumerate(outs):
            start = ((g + k) & 3) * QUART
            for t in range(QUART):
                out[t] = final[start + t]


def call_pairs(sources, target, tables, before=None, ends=None):
    kinds = tuple(len(same) for same, _ in sources)
    last = ends is not None
    operands = [v for same, other in sources for v in list(same) + list(other)]
    operands += [target, *tables] + ([] if before is None else [before]) + list(ends or [])
    scratch = [
        pltpu.VMEM((N, N, LANES), BF),
        pltpu.VMEM((N * PITCH, LANES), F32),
        pltpu.VMEM((N * PITCH, LANES), F32),
        pltpu.VMEM((len(kinds) * TILES, N, LANES), BF),
        pltpu.VMEM((SLAB * REST, LANES), F32),
    ]
    if last:
        scratch += [pltpu.VMEM((N, N, LANES), F32), pltpu.VMEM((TILES + 2, N, LANES), BF)]
    return pl.pallas_call(
        functools.partial(pairs_kernel, kinds, before is None, last),
        out_shape=tuple(shape((QUART, N, LANES)) for _ in range(4)) if last else shape((N, N, LANES), F32),
        in_specs=[VM] * len(operands),
        out_specs=(VM,) * 4 if last else VM,
        scratch_shapes=scratch,
        compiler_params=LARGE,
        cost_estimate=pl.CostEstimate(
            flops=6_000_000_000 * len(kinds), bytes_accessed=8_000_000, transcendentals=0
        ),
    )(*operands)


def select_kernel(own, got1, got2, got3, sel_t, msg, scr):
    tables = [sel_t[c] for c in range(SLOTS)]
    for t in range(QUART):
        total = (
            own[t].astype(F32) + got1[t].astype(F32) + got2[t].astype(F32) + got3[t].astype(F32)
        ).astype(BF)
        for c in range(SLOTS):
            scr[(c * QUART + t) * BANDS : (c * QUART + t + 1) * BANDS, :] = dot(tables[c], total)

    def body(d, _):
        msg[d] = scr[pl.ds(d, ROWS_T, stride=BANDS), :].astype(BF)
        return 0

    lax.fori_loop(0, BANDS, body, 0, unroll=8)


def rows_out_kernel(got, low, high, scr):
    def load(b, _):
        scr[pl.ds(pl.multiple_of(b * ROWS_T, 8), ROWS_T), :] = got[b].astype(F32)
        return 0

    lax.fori_loop(0, BANDS, load, 0, unroll=8)
    for c in range(SLOTS):
        for t in range(QUART):
            rows = scr[pl.ds(c * QUART + t, BANDS, stride=ROWS_T), :].astype(BF)
            low[c, :, t * LANES : (t + 1) * LANES] = rows[:HALF]
            high[c, :, t * LANES : (t + 1) * LANES] = rows[HALF:]


def join_kernel(*refs):
    out = refs[8]
    g = lax.axis_index("grp")
    wide = QUART * LANES
    short = (TILES - 3 * QUART) * LANES
    for k in range(4):
        origin = (g - k) & 3
        start = pl.multiple_of(origin * wide, LANES)

        @pl.when(origin < 3)
        def _():
            for c in range(SLOTS):
                for e in range(2):
                    out[c, e * HALF : (e + 1) * HALF, pl.ds(start, wide)] = refs[2 * k + e][c]

        @pl.when(origin == 3)
        def _():
            for c in range(SLOTS):
                for e in range(2):
                    out[c, e * HALF : (e + 1) * HALF, 3 * wide :] = refs[2 * k + e][c, :, :short]


VM = pl.BlockSpec(memory_space=pltpu.VMEM)
HB = pl.BlockSpec(memory_space=pltpu.HBM)
PARAMS = pltpu.CompilerParams(vmem_limit_bytes=16 * 1024 * 1024)
WHOLE_VMEM = pltpu.CompilerParams(vmem_limit_bytes=60 * 1024 * 1024)
LARGE = pltpu.CompilerParams(vmem_limit_bytes=30 * 1024 * 1024)


def shape(dims, kind=BF):
    return jax.ShapeDtypeStruct(dims, kind)


def shift_grp(value, k):
    return lax.ppermute(value, "grp", [(i, (i + k) % GROUPS) for i in range(GROUPS)])


def swap_band(value, axis):
    bit = {"core": 1, "z": 2}[axis]
    return lax.ppermute(value, "band", [(i, i ^ bit) for i in range(BANDS)])


def shift_band(value, dx, dz, dc):
    moves = []
    for x in range(4):
        for z in range(8):
            for c in range(2):
                there = (((x + dx) % 4) * 8 + (z + dz) % 8) * 2 + (c + dc) % 2
                moves.append(((x * 8 + z) * 2 + c, there))
    return lax.ppermute(value, "band", moves)


def ring_gather(first, second, step):
    ahead = step(first, 1), step(second, 1)
    behind = step(first, 3), step(second, 3)
    far = step(ahead[0], 1), step(behind[1], 3)
    return [(first, second), ahead, far, behind]


def shards(stick_data, row_lengths, row_order, source_order):
    table = jnp.asarray(hartley_table())
    expand = jnp.asarray(expand_tables(hartley_table()))
    twin = jnp.asarray(pair_table(hartley_table()))
    c0, c1, c2 = (jnp.asarray(v) for v in compress_tables(hartley_table()))
    screen = jnp.asarray(screen_table())

    msg = pl.pallas_call(
        pack_kernel,
        out_shape=shape((BANDS, ROWS_M, LANES)),
        in_specs=[HB] * 2,
        out_specs=VM,
        scratch_shapes=[
            pltpu.SMEM((BANDS,), jnp.int32),
            pltpu.VMEM((SLOTS, BANDS, TILES * LANES), BF),
            pltpu.VMEM((ROWS_T * BANDS, LANES), F32),
            pltpu.VMEM((BANDS * ROWS_S, LANES), F32),
            pltpu.SemaphoreType.DMA((2,)),
        ],
        compiler_params=WHOLE_VMEM,
    )(source_order, stick_data)
    got = lax.all_to_all(msg, "band", 0, 0, tiled=True)
    quarter, piece, sel_t = pl.pallas_call(
        rows_kernel,
        out_shape=(shape((QUART, N, LANES)), shape((PIECE, LANES)), shape((SLOTS, BANDS, N))),
        in_specs=[VM] * 4,
        out_specs=(VM,) * 3,
        scratch_shapes=[
            pltpu.VMEM((ROWS_M * BANDS, LANES), F32),
            pltpu.VMEM((N + 16, LANES), F32),
        ],
        compiler_params=PARAMS,
    )(got, row_lengths.reshape(1, BANDS), row_order.reshape(1, N), table)

    swapped = swap_band(piece, "z")
    couple = jnp.stack([piece, swapped])
    behind_one, opposite, before_one = (shift_grp(quarter, k) for k in (1, 2, 3))
    again, behind_one = lax.optimization_barrier((couple, behind_one))
    others = shift_band(couple, 0, 2, 0), shift_band(couple, 0, 4, 0), shift_band(again, 0, 6, 0)
    along_z = jnp.stack([couple, *others])
    quarters = [quarter, behind_one, opposite, before_one]
    along_z, *quarters = lax.optimization_barrier((along_z, *quarters))

    target = pl.pallas_call(
        target_kernel,
        out_shape=shape((N, N, LANES)),
        in_specs=[VM] * 6,
        out_specs=VM,
        scratch_shapes=[
            pltpu.VMEM((N * PITCH, LANES), F32),
            pltpu.VMEM((4 * QUART, N, LANES), BF),
        ],
        compiler_params=PARAMS,
    )(*quarters, table, expand)

    ahead, behind = shift_band(along_z, 1, 0, 0), shift_band(along_z, 3, 0, 0)
    flip = lambda v: shift_band(v, 0, 0, 1)

    tables = (table, expand, twin, screen)
    partial = call_pairs([([along_z], [flip(along_z)])], target, tables)
    ahead, behind, partial = lax.optimization_barrier((ahead, behind, partial))
    far = shift_band(ahead[:2], 1, 0, 0), shift_band(behind[2:], 3, 0, 0)
    ahead_flip, behind_flip = flip(ahead), flip(behind)
    partial = call_pairs([([ahead], [ahead_flip])], target, tables, before=partial)
    far_a, far_b, partial = lax.optimization_barrier((*far, partial))
    far, far_flip = (far_a, far_b), [flip(far_a), flip(far_b)]
    partial = call_pairs([([behind], [behind_flip])], target, tables, before=partial)
    outs = call_pairs([(far, far_flip)], target, tables, before=partial, ends=(c0, c1, c2))

    parts = [outs[0]] + [shift_grp(outs[k], k) for k in (2, 1, 3)]
    message = pl.pallas_call(
        select_kernel,
        out_shape=shape((BANDS, ROWS_T, LANES)),
        in_specs=[VM] * 5,
        out_specs=VM,
        scratch_shapes=[pltpu.VMEM((ROWS_T * BANDS, LANES), F32)],
        compiler_params=PARAMS,
    )(*parts, sel_t)

    received = lax.all_to_all(message, "band", 0, 0, tiled=True)
    low, high = pl.pallas_call(
        rows_out_kernel,
        out_shape=(shape((SLOTS, HALF, QUART * LANES)),) * 2,
        in_specs=[VM],
        out_specs=(VM, VM),
        scratch_shapes=[pltpu.VMEM((ROWS_T * BANDS, LANES), F32)],
        compiler_params=PARAMS,
    )(received)

    spread = ring_gather(low, high, shift_grp)
    return pl.pallas_call(
        join_kernel,
        out_shape=shape((SLOTS, BANDS, TILES * LANES)),
        in_specs=[VM] * 8,
        out_specs=VM,
        compiler_params=PARAMS,
    )(*[v for both in spread for v in both])


def solution(mesh):
    return jax.shard_map(
        shards,
        mesh=mesh,
        in_specs=(P("band", None, None), P(), P(), P()),
        out_specs=P("band", None, None),
        check_vma=False,
    )
```

```python
import functools
import math

import jax
import jax.numpy as jnp
import numpy as np
from jax import lax
from jax.experimental import pallas as pl
from jax.experimental.pallas import tpu as pltpu
from jax.sharding import PartitionSpec as P

N = 80
LANES = 128
TILES = 50
QUART = 13
SRC = 4
SLOTS = 3
BANDS = 64
GROUPS = 4
ROWS_T = 40
ROWS_S = 16
EACH = 3
SLAB = 16
WHOLE = EACH * SLAB
REST = 10
PIECE = 256
ROWS_M = ROWS_T + ROWS_S
HALF = BANDS // 2
PITCH = 88
BF = jnp.bfloat16
F32 = jnp.float32

coulomb_peak = 4.0
screen_square = 64.0


def hartley_table():
    index = np.arange(N)
    angles = (index[:, None] * index[None, :] % N).astype(np.float32) * np.float32(2.0 * math.pi / N)
    return ((np.cos(angles) + np.sin(angles)) / np.float32(math.sqrt(N))).astype(BF)


def expand_tables(table):
    out = np.zeros((4, 256, 256), BF)
    for p in range(4):
        off = 160 * p % LANES
        out[p, off : off + N, :N] = table
        out[p, off + N : off + 2 * N, LANES : LANES + N] = table
    return out


def pair_table(table):
    out = np.zeros((256, 256), BF)
    out[:N, :N] = table
    out[LANES : LANES + N, LANES : LANES + N] = table
    return out


def compress_tables(table):
    whole = np.zeros((1024, 640), BF)
    for y in range(8):
        whole[y * LANES : y * LANES + N, y * N : (y + 1) * N] = table
    return whole[:512, :256].copy(), whole[384:896, 256:512].copy(), whole[768:, 512:].copy()


def screen_table():
    freq = np.minimum(np.arange(N), N - np.arange(N)).astype(np.float32)
    sq = freq * freq
    total = sq[:41, None, None] + sq[None, :, None] + sq[None, None, :]
    out = np.zeros((41, N, LANES), np.float32)
    out[:, :, :N] = np.float32(coulomb_peak) / (np.float32(1.0) + total / np.float32(screen_square))
    return out


def dot(a, b):
    return jnp.dot(a, b, preferred_element_type=F32)


def dot_tn(a, b):
    return lax.dot_general(a, b, (((0,), (0,)), ((), ())), preferred_element_type=F32)


def pack_kernel(
    order_h, stick_h, msg, order_s, stick, scr, scr_s, sem,
):
    slots = [pltpu.make_async_copy(stick_h.at[c], stick.at[c], sem.at[c]) for c in range(SLOTS)]
    order = pltpu.make_async_copy(order_h, order_s, sem.at[SLOTS])
    order.start()
    for copy in slots:
        copy.start()
    order.wait()
    g = lax.axis_index("grp")
    b1 = lax.broadcasted_iota(jnp.int32, (16, BANDS), 1)
    r1 = lax.broadcasted_iota(jnp.int32, (16, BANDS), 0)
    pick = jnp.zeros((16, BANDS), F32)
    for k in range(SRC):
        pick = jnp.where((r1 == k) & (b1 == order_s[g * SRC + k]), 1.0, pick)
    pick = pick.astype(BF)
    first = QUART * g
    for c in range(SLOTS):
        slots[c].wait()
        for t in range(QUART):
            lane = pl.multiple_of(jnp.minimum(first + t, TILES - 1) * LANES, LANES)
            row = (c * QUART + t) * BANDS
            scr[row : row + BANDS, :] = stick[c, :, pl.ds(lane, LANES)].astype(F32)
        for u in range(TILES // 2):
            got = dot(pick, stick[c, :, u * 256 : u * 256 + 256])
            for h in range(2):
                for k in range(SRC):
                    t = 2 * u + h
                    line = got[k : k + 1, h * LANES : (h + 1) * LANES]
                    if t < WHOLE:
                        places = [(t // EACH, t % EACH)]
                    else:
                        places = [(8 * (t - WHOLE) + i, EACH) for i in range(8)]
                    for d, r in places:
                        row = (k * SLAB + d) * ROWS_S + c * SRC + r
                        scr_s[row : row + 1, :] = line

    def out_body(b, _):
        mine = scr[pl.ds(b, ROWS_T, stride=BANDS), :]
        tile = scr_s[pl.ds(pl.multiple_of(b * ROWS_S, 8), ROWS_S), :]
        msg[b] = jnp.concatenate([mine, tile], axis=0).astype(BF)
        return 0

    lax.fori_loop(0, BANDS, out_body, 0, unroll=8)


def rows_kernel(got, lengths, order_v, table, quarter, piece, sel_t, scr, last):
    lens = lengths[...]
    d0 = lax.broadcasted_iota(jnp.int32, (BANDS, BANDS), 0)
    d1 = lax.broadcasted_iota(jnp.int32, (BANDS, BANDS), 1)
    before = jnp.where(d0 < d1, 1.0, 0.0).astype(BF)
    lens8 = jnp.broadcast_to(lens, (8, BANDS)).astype(F32)
    starts = dot(lens8.astype(BF), before)[:1]
    q0 = lax.broadcasted_iota(jnp.int32, (N, N), 0)
    perm = jnp.where(jnp.broadcast_to(order_v[...], (N, N)) == q0, 1.0, 0.0).astype(BF)
    permuted = dot(table[...], perm).astype(BF)
    place = lax.broadcasted_iota(jnp.int32, (N, BANDS), 0).astype(F32)
    tables = []
    for c in range(SLOTS):
        hit = (place == jnp.broadcast_to(starts + c, (N, BANDS))) & (
            jnp.broadcast_to(lens8[:1], (N, BANDS)) > c
        )
        one = jnp.where(hit, 1.0, 0.0).astype(BF)
        tables.append(dot(permuted, one).astype(BF))
        sel_t[c] = lax.dot_general(
            one, permuted, (((0,), (1,)), ((), ())), preferred_element_type=F32
        ).astype(BF)
    def load(d, _):
        scr[pl.ds(pl.multiple_of(d * ROWS_M, 8), ROWS_M), :] = got[d].astype(F32)
        return 0

    lax.fori_loop(0, BANDS, load, 0, unroll=8)

    def contracted(first, count, t):
        total = jnp.zeros((N, LANES), F32)
        for c in range(SLOTS):
            rows = scr[pl.ds(first + c * count + t, BANDS, stride=ROWS_M), :].astype(BF)
            total = total + dot(tables[c], rows)
        return total

    for r in range(EACH):
        piece[r * N : (r + 1) * N, :] = contracted(ROWS_T, SRC, r).astype(BF)
    last[:N, :] = contracted(ROWS_T, SRC, EACH)
    last[N:, :] = jnp.zeros((16, LANES), F32)
    band = lax.axis_index("band")
    piece[EACH * N :, :] = last[pl.ds((band & 7) * REST, 16), :].astype(BF)
    for t in range(QUART):
        quarter[t] = contracted(0, QUART, t).astype(BF)


def turned(scr, index):
    return jnp.concatenate(
        [
            scr[pl.ds(index, N, stride=PITCH), :].astype(BF),
            scr[pl.ds(index + 1, N, stride=PITCH), :].astype(BF),
        ],
        axis=1,
    )


def put(scr, index, values):
    scr[index * PITCH : index * PITCH + N, :] = values[:, :LANES]
    scr[(index + 1) * PITCH : (index + 1) * PITCH + N, :] = values[:, LANES:]


def side(ref, index):
    return jnp.concatenate([ref[index], ref[index + 1]], axis=1)


CHUNK = 5


def to_real(tile, out, table, expand, scr):
    for p in range(4):
        for lead in range(0, 10, CHUNK):
            rows = []
            for i in range(lead, lead + CHUNK):
                a = i * 5 + (160 * p) // LANES
                rows.append(jnp.concatenate([tile(a), tile(a + 1)], axis=1))
            res = dot(jnp.concatenate(rows, axis=0), expand[p])
            for j in range(CHUNK):
                put(scr, (lead + j) * 8 + 2 * p, res[j * N : (j + 1) * N])
    h = table[...]
    for x in range(0, N, 2):
        res = dot(h, turned(scr, x)).astype(BF)
        out[x] = res[:, :LANES]
        out[x + 1] = res[:, LANES:]


def target_kernel(own, got1, got2, got3, table, expand, out, scr, quarters):
    g = lax.axis_index("grp")
    for k, ref in enumerate((own, got1, got2, got3)):
        start = ((g - k) & 3) * QUART
        for t in range(QUART):
            quarters[start + t] = ref[t]
    to_real(lambda t: quarters[t], out, table, expand, scr)


PLACES = [(back, swap) for back in (0, 2, 4, 6) for swap in (False, True)]


def gather_tiles(same, other, pieces, lead, rest):
    band = lax.axis_index("band")
    core, z_at = band & 1, (band >> 1) & 7
    for refs, flip in ((same, 0), (other, 1)):
        couples = [ref.at[i] for ref in refs for i in range(ref.shape[0])]
        for j, (back, swap) in enumerate(PLACES):
            z = (z_at - back) & 7
            z = (z ^ 1) if swap else z
            origin = z * 2 + (core ^ flip)
            whole = couples[j // 2][j % 2]
            for r in range(EACH):
                pieces[lead + origin * EACH + r] = whole[r * N : (r + 1) * N]
            rest[pl.ds(origin * REST, REST), :] = whole[EACH * N :].astype(F32)[:REST]
    for j in range(TILES - WHOLE):
        pieces[lead + WHOLE + j] = rest[j * N : (j + 1) * N, :].astype(BF)


def one_source(pieces, k, target, source, before, partial, table, expand, twin, screen, scr_a, scr_b):
    to_real(lambda t: pieces[k * TILES + t], source, table, expand, scr_a)
    h = table[...]
    turn = twin[...]
    for lead in range(0, N, 2 * CHUNK):
        rows = []
        for x in range(lead, lead + 2 * CHUNK, 2):
            rows.append(dot(h, side(target, x) * side(source, x)).astype(BF))
        res = dot(jnp.concatenate(rows, axis=0), turn)
        for j in range(CHUNK):
            put(scr_a, lead + 2 * j, res[j * N : (j + 1) * N])
    for y in range(0, N, 2):
        spec = dot(h, turned(scr_a, y))
        weight = jnp.concatenate([screen[min(y, N - y)], screen[min(y + 1, N - 1 - y)]], axis=1)
        put(scr_b, y, dot(h, (spec * weight).astype(BF)))
    for lead in range(0, N, 2 * CHUNK):
        rows = [turned(scr_b, x) for x in range(lead, lead + 2 * CHUNK, 2)]
        res = dot(jnp.concatenate(rows, axis=0), turn).astype(BF)
        for j in range(CHUNK):
            pot = dot(h, res[j * N : (j + 1) * N])
            for e in range(2):
                x = lead + 2 * j + e
                term = source[x].astype(F32) * pot[:, e * LANES : (e + 1) * LANES]
                partial[x] = term if before is None else before[x] + term


def last_transform(partial, table, c0, c1, c2, scr, final):
    h = table[...]
    for x in range(0, N, 2):
        put(scr, x, dot(h, side(partial, x).astype(BF)))
    blocks = [[turned(scr, y + 2 * p) for p in range(4)] for y in range(0, N, 8)]
    for i in range(0, 10, CHUNK):
        eights = [jnp.concatenate(blocks[i + j], axis=1) for j in range(CHUNK)]
        r0 = dot(jnp.concatenate([v[:, :512] for v in eights], axis=0), c0[...]).astype(BF)
        r1 = dot(jnp.concatenate([v[:, 384:896] for v in eights], axis=0), c1[...]).astype(BF)
        r2 = dot(jnp.concatenate([v[:, 768:] for v in eights], axis=0), c2[...]).astype(BF)
        for j in range(CHUNK):
            t = (i + j) * 5
            rows = slice(j * N, (j + 1) * N)
            final[t] = r0[rows, :LANES]
            final[t + 1] = r0[rows, LANES:]
            final[t + 2] = r1[rows, :LANES]
            final[t + 3] = r1[rows, LANES:]
            final[t + 4] = r2[rows]
    final[TILES] = jnp.zeros((N, LANES), BF)
    final[TILES + 1] = jnp.zeros((N, LANES), BF)


def pairs_kernel(kinds, first, last, *refs):
    refs = list(refs)
    take = lambda n: [refs.pop(0) for _ in range(n)]
    sources = [(take(n), take(n)) for n in kinds]
    target, table, expand, twin, screen = take(5)
    before = None if first else take(1)[0]
    tables = take(3) if last else []
    outs = take(4) if last else take(1)
    source, scr_a, scr_b, pieces, rest = take(5)
    partial, final = take(2) if last else (outs[0], None)
    for i, (same, other) in enumerate(sources):
        gather_tiles(same, other, pieces, i * TILES, rest)
    work = (table, expand, twin, screen, scr_a, scr_b)
    if len(kinds) == 1:
        one_source(pieces, 0, target, source, before, partial, *work)
    else:
        partial[...] = before[...]

        def body(k, _):
            one_source(pieces, k, target, source, partial, partial, *work)
            return 0

        lax.fori_loop(0, len(kinds), body, 0)
    if last:
        last_transform(partial, table, *tables, scr_a, final)
        g = lax.axis_index("grp")
        for k, out in enumerate(outs):
            start = ((g + k) & 3) * QUART
            for t in range(QUART):
                out[t] = final[start + t]


def call_pairs(sources, target, tables, before=None, ends=None):
    kinds = tuple(len(same) for same, _ in sources)
    last = ends is not None
    operands = [v for same, other in sources for v in list(same) + list(other)]
    operands += [target, *tables] + ([] if before is None else [before]) + list(ends or [])
    scratch = [
        pltpu.VMEM((N, N, LANES), BF),
        pltpu.VMEM((N * PITCH, LANES), F32),
        pltpu.VMEM((N * PITCH, LANES), F32),
        pltpu.VMEM((len(kinds) * TILES, N, LANES), BF),
        pltpu.VMEM((SLAB * REST, LANES), F32),
    ]
    if last:
        scratch += [pltpu.VMEM((N, N, LANES), F32), pltpu.VMEM((TILES + 2, N, LANES), BF)]
    return pl.pallas_call(
        functools.partial(pairs_kernel, kinds, before is None, last),
        out_shape=tuple(shape((QUART, N, LANES)) for _ in range(4)) if last else shape((N, N, LANES), F32),
        in_specs=[VM] * len(operands),
        out_specs=(VM,) * 4 if last else VM,
        scratch_shapes=scratch,
        compiler_params=LARGE,
        cost_estimate=pl.CostEstimate(
            flops=6_000_000_000 * len(kinds), bytes_accessed=8_000_000, transcendentals=0
        ),
    )(*operands)


def select_kernel(own, got1, got2, got3, sel_t, msg, scr):
    tables = [sel_t[c] for c in range(SLOTS)]
    for t in range(QUART):
        total = (
            own[t].astype(F32) + got1[t].astype(F32) + got2[t].astype(F32) + got3[t].astype(F32)
        ).astype(BF)
        for c in range(SLOTS):
            scr[(c * QUART + t) * BANDS : (c * QUART + t + 1) * BANDS, :] = dot(tables[c], total)

    def body(d, _):
        msg[d] = scr[pl.ds(d, ROWS_T, stride=BANDS), :].astype(BF)
        return 0

    lax.fori_loop(0, BANDS, body, 0, unroll=8)


def rows_out_kernel(got, low, high, scr):
    def load(b, _):
        scr[pl.ds(pl.multiple_of(b * ROWS_T, 8), ROWS_T), :] = got[b].astype(F32)
        return 0

    lax.fori_loop(0, BANDS, load, 0, unroll=8)
    for c in range(SLOTS):
        for t in range(QUART):
            rows = scr[pl.ds(c * QUART + t, BANDS, stride=ROWS_T), :].astype(BF)
            low[c, :, t * LANES : (t + 1) * LANES] = rows[:HALF]
            high[c, :, t * LANES : (t + 1) * LANES] = rows[HALF:]


def join_kernel(*refs):
    out = refs[8]
    g = lax.axis_index("grp")
    wide = QUART * LANES
    short = (TILES - 3 * QUART) * LANES
    for k in range(4):
        origin = (g - k) & 3
        start = pl.multiple_of(origin * wide, LANES)

        @pl.when(origin < 3)
        def _():
            for c in range(SLOTS):
                for e in range(2):
                    out[c, e * HALF : (e + 1) * HALF, pl.ds(start, wide)] = refs[2 * k + e][c]

        @pl.when(origin == 3)
        def _():
            for c in range(SLOTS):
                for e in range(2):
                    out[c, e * HALF : (e + 1) * HALF, 3 * wide :] = refs[2 * k + e][c, :, :short]


VM = pl.BlockSpec(memory_space=pltpu.VMEM)
HB = pl.BlockSpec(memory_space=pltpu.HBM)
PARAMS = pltpu.CompilerParams(vmem_limit_bytes=16 * 1024 * 1024)
WHOLE_VMEM = pltpu.CompilerParams(vmem_limit_bytes=60 * 1024 * 1024)
LARGE = pltpu.CompilerParams(vmem_limit_bytes=30 * 1024 * 1024)


def shape(dims, kind=BF):
    return jax.ShapeDtypeStruct(dims, kind)


def shift_grp(value, k):
    return lax.ppermute(value, "grp", [(i, (i + k) % GROUPS) for i in range(GROUPS)])


def swap_band(value, axis):
    bit = {"core": 1, "z": 2}[axis]
    return lax.ppermute(value, "band", [(i, i ^ bit) for i in range(BANDS)])


def shift_band(value, dx, dz, dc):
    moves = []
    for x in range(4):
        for z in range(8):
            for c in range(2):
                there = (((x + dx) % 4) * 8 + (z + dz) % 8) * 2 + (c + dc) % 2
                moves.append(((x * 8 + z) * 2 + c, there))
    return lax.ppermute(value, "band", moves)


def ring_gather(first, second, step):
    ahead = step(first, 1), step(second, 1)
    behind = step(first, 3), step(second, 3)
    far = step(ahead[0], 1), step(behind[1], 3)
    return [(first, second), ahead, far, behind]


def shards(stick_data, row_lengths, row_order, source_order):
    table = jnp.asarray(hartley_table())
    expand = jnp.asarray(expand_tables(hartley_table()))
    twin = jnp.asarray(pair_table(hartley_table()))
    c0, c1, c2 = (jnp.asarray(v) for v in compress_tables(hartley_table()))
    screen = jnp.asarray(screen_table())

    msg = pl.pallas_call(
        pack_kernel,
        out_shape=shape((BANDS, ROWS_M, LANES)),
        in_specs=[HB] * 2,
        out_specs=VM,
        scratch_shapes=[
            pltpu.SMEM((BANDS,), jnp.int32),
            pltpu.VMEM((SLOTS, BANDS, TILES * LANES), BF),
            pltpu.VMEM((ROWS_T * BANDS, LANES), F32),
            pltpu.VMEM((BANDS * ROWS_S, LANES), F32),
            pltpu.SemaphoreType.DMA((SLOTS + 1,)),
        ],
        compiler_params=WHOLE_VMEM,
    )(source_order, stick_data)
    got = lax.all_to_all(msg, "band", 0, 0, tiled=True)
    quarter, piece, sel_t = pl.pallas_call(
        rows_kernel,
        out_shape=(shape((QUART, N, LANES)), shape((PIECE, LANES)), shape((SLOTS, BANDS, N))),
        in_specs=[VM] * 4,
        out_specs=(VM,) * 3,
        scratch_shapes=[
            pltpu.VMEM((ROWS_M * BANDS, LANES), F32),
            pltpu.VMEM((N + 16, LANES), F32),
        ],
        compiler_params=PARAMS,
    )(got, row_lengths.reshape(1, BANDS), row_order.reshape(1, N), table)

    swapped = swap_band(piece, "z")
    couple = jnp.stack([piece, swapped])
    behind_one, opposite, before_one = (shift_grp(quarter, k) for k in (1, 2, 3))
    again, behind_one = lax.optimization_barrier((couple, behind_one))
    others = shift_band(couple, 0, 2, 0), shift_band(couple, 0, 4, 0), shift_band(again, 0, 6, 0)
    along_z = jnp.stack([couple, *others])
    quarters = [quarter, behind_one, opposite, before_one]
    along_z, *quarters = lax.optimization_barrier((along_z, *quarters))

    target = pl.pallas_call(
        target_kernel,
        out_shape=shape((N, N, LANES)),
        in_specs=[VM] * 6,
        out_specs=VM,
        scratch_shapes=[
            pltpu.VMEM((N * PITCH, LANES), F32),
            pltpu.VMEM((4 * QUART, N, LANES), BF),
        ],
        compiler_params=PARAMS,
    )(*quarters, table, expand)

    ahead, behind = shift_band(along_z, 1, 0, 0), shift_band(along_z, 3, 0, 0)
    flip = lambda v: shift_band(v, 0, 0, 1)

    tables = (table, expand, twin, screen)
    partial = call_pairs([([along_z], [flip(along_z)])], target, tables)
    ahead, behind, partial = lax.optimization_barrier((ahead, behind, partial))
    far = shift_band(ahead[:2], 1, 0, 0), shift_band(behind[2:], 3, 0, 0)
    ahead_flip, behind_flip = flip(ahead), flip(behind)
    partial = call_pairs([([ahead], [ahead_flip])], target, tables, before=partial)
    far_a, far_b, partial = lax.optimization_barrier((*far, partial))
    far, far_flip = (far_a, far_b), [flip(far_a), flip(far_b)]
    partial = call_pairs([([behind], [behind_flip])], target, tables, before=partial)
    outs = call_pairs([(far, far_flip)], target, tables, before=partial, ends=(c0, c1, c2))

    parts = [outs[0]] + [shift_grp(outs[k], k) for k in (2, 1, 3)]
    message = pl.pallas_call(
        select_kernel,
        out_shape=shape((BANDS, ROWS_T, LANES)),
        in_specs=[VM] * 5,
        out_specs=VM,
        scratch_shapes=[pltpu.VMEM((ROWS_T * BANDS, LANES), F32)],
        compiler_params=PARAMS,
    )(*parts, sel_t)

    received = lax.all_to_all(message, "band", 0, 0, tiled=True)
    low, high = pl.pallas_call(
        rows_out_kernel,
        out_shape=(shape((SLOTS, HALF, QUART * LANES)),) * 2,
        in_specs=[VM],
        out_specs=(VM, VM),
        scratch_shapes=[pltpu.VMEM((ROWS_T * BANDS, LANES), F32)],
        compiler_params=PARAMS,
    )(received)

    spread = ring_gather(low, high, shift_grp)
    return pl.pallas_call(
        join_kernel,
        out_shape=shape((SLOTS, BANDS, TILES * LANES)),
        in_specs=[VM] * 8,
        out_specs=VM,
        compiler_params=PARAMS,
    )(*[v for both in spread for v in both])


def solution(mesh):
    return jax.shard_map(
        shards,
        mesh=mesh,
        in_specs=(P("band", None, None), P(), P(), P()),
        out_specs=P("band", None, None),
        check_vma=False,
    )
```
